512 devices in a mesh: gx: 4 (over x), gy: 8 (over z_lo, core), gz: 16 (over z_hi, y).
Axes of the slice: x: 4, y: 4, z: 16 (z_hi: 4, z_lo: 4; z = z_hi * 4 + z_lo), core: 2. Of those that a mesh axis runs over, the one named last changes fastest.
Arguments:
- offsets: float32 [3, 8, 16, 32, 16], P(None, 'gx', 'gy', 'gz'), may hold values from 0 to 6
- species: int32 [8, 16, 32, 16], P('gx', 'gy', 'gz'), may hold values from 0 to 88
- counts: int32 [8, 16, 32], P('gx', 'gy', 'gz'), may hold values from 2 to 16, as said below
- edges: int32 [2, 4, 8, 16, 1024], P(None, 'gx', 'gy', 'gz'), may hold values from -1 to 1023, as said below
- emb: bfloat16 [89, 128], replicated, may hold values from -6 to 6
- rad_in: bfloat16 [2, 8, 64], replicated, may hold values from -2 to 2
- rad_hid: bfloat16 [2, 64, 64], replicated, may hold values from -0.75 to 0.75
- rad_out: bfloat16 [2, 64, 256], replicated, may hold values from -0.75 to 0.75
- mix_one: bfloat16 [2, 128, 128], replicated, may hold values from -0.5 to 0.5
- project: bfloat16 [2, 128, 128], replicated, may hold values from -0.5 to 0.5
- mix_two: bfloat16 [128, 128], replicated, may hold values from -0.5 to 0.5
- readout: float32 [128], replicated, may hold values from -0.5 to 0.5
Outputs:
- forces: float32 [3, 8, 16, 32, 16], P(None, 'gx', 'gy', 'gz')
- energy: float32 [], replicated
The draws below stay inside these ranges and needn't reach their ends.
Inputs may be any that keep to these rules, and one draw needn't show every extreme that they name: `counts`: every cell holds 2 to 16 atoms, in its lowest slots; some cell holds exactly 16. `edges`: each occupied slot of a device's cells is the target of exactly 8 entries, in random order; other entries are -1 in both rows. A source is an occupied slot of the target's cell or of one of its 26 neighbouring cells, never the target itself, and may repeat.
All inputs are finite; a program needn't handle non-finite values.
Results may differ from the reference program's by a relative error of at most 0.015.
Values may be sent and summed in bfloat16 or wider, within the bound.
A program may use at most 128 MiB of HBM per device.

```python
import jax
import jax.numpy as jnp
from jax import lax

C = 128
NSPEC = 89
RH = 64
NB = 8
S = 16
DEG = 8
KX = 2
KY = 2
KZ = 2
GX = 8
GY = 16
GZ = 32
E_DEV = 1024
N_GX = 4
N_GY = 8
N_GZ = 16


def cell_counts(key):
    count_key = jax.random.fold_in(key, 7)
    z_index = jnp.arange(GZ, dtype=jnp.int32)
    third_slots = S // 3
    upper_count = jnp.maximum(third_slots + (S - third_slots) * z_index // max(GZ - 1, 1), 2)
    lower_count = jnp.maximum(upper_count // 2, 2)
    raw_bits = jax.random.randint(count_key, (GX, GY, GZ), 0, 1 << 20, dtype=jnp.int32)
    result = lower_count[None, None, :] + raw_bits % (upper_count - lower_count + 1)[None, None, :]
    index_x = lax.broadcasted_iota(jnp.int32, (GX, GY, GZ), 0)
    index_y = lax.broadcasted_iota(jnp.int32, (GX, GY, GZ), 1)
    index_z = lax.broadcasted_iota(jnp.int32, (GX, GY, GZ), 2)
    full_cell = (index_x == 0) & (index_y == 0) & (index_z == GZ - 1)
    return jnp.where(full_cell, S, result).astype(jnp.int32)


def draw_counts(key, part):
    return cell_counts(key)


def draw_edges(key, part):
    cell_load = cell_counts(key)
    across_x = GX // KX
    across_y = GY // KY
    across_z = GZ // KZ
    edge_key = jax.random.fold_in(key, 13)
    first_key, second_key, third_key = jax.random.split(edge_key, 3)
    shape = (across_x, across_y, across_z, KX, KY, KZ, S, DEG)
    device_x = lax.broadcasted_iota(jnp.int32, shape, 0)
    device_y = lax.broadcasted_iota(jnp.int32, shape, 1)
    device_z = lax.broadcasted_iota(jnp.int32, shape, 2)
    cell_x = lax.broadcasted_iota(jnp.int32, shape, 3)
    cell_y = lax.broadcasted_iota(jnp.int32, shape, 4)
    cell_z = lax.broadcasted_iota(jnp.int32, shape, 5)
    slot_index = lax.broadcasted_iota(jnp.int32, shape, 6)
    global_x = device_x * KX + cell_x
    global_y = device_y * KY + cell_y
    global_z = device_z * KZ + cell_z
    occupied = slot_index < cell_load[global_x, global_y, global_z]
    neighbour = jax.random.randint(first_key, shape, 0, 27, dtype=jnp.int32)
    offset_x = neighbour // 9
    offset_y = neighbour // 3 % 3
    offset_z = neighbour % 3
    source_x = (global_x + offset_x - 1) % GX
    source_y = (global_y + offset_y - 1) % GY
    source_z = (global_z + offset_z - 1) % GZ
    source_load = cell_load[source_x, source_y, source_z]
    raw_bits = jax.random.randint(second_key, shape, 0, 1 << 20, dtype=jnp.int32)
    centre = neighbour == 13
    other_slot = (slot_index + 1 + raw_bits % jnp.maximum(source_load - 1, 1)) % source_load
    source_slot = jnp.where(centre, other_slot, raw_bits % source_load)
    target = jnp.where(occupied, ((cell_x * KY + cell_y) * KZ + cell_z) * S + slot_index, -1)
    padded_index = (((cell_x + offset_x) * (KY + 2) + (cell_y + offset_y)) * (KZ + 2) + (cell_z + offset_z)) * S + source_slot
    source = jnp.where(occupied, padded_index, -1)
    device_total = across_x * across_y * across_z
    target = target.reshape(device_total, E_DEV)
    source = source.reshape(device_total, E_DEV)
    device_keys = jax.random.split(third_key, device_total)
    shuffle = jax.vmap(lambda device_key: jax.random.permutation(device_key, E_DEV))(device_keys)
    target = jnp.take_along_axis(target, shuffle, axis=1)
    source = jnp.take_along_axis(source, shuffle, axis=1)
    return jnp.stack([target, source], axis=0).reshape(2, across_x, across_y, across_z, E_DEV).astype(jnp.int32)


def touch_ends(array, own_key, smallest, largest):
    spot = [jax.random.randint(jax.random.fold_in(own_key, axis), (), 0, length) for axis, length in enumerate(array.shape)]
    longest = array.shape.index(max(array.shape))
    next_to = spot[:longest] + [(spot[longest] + 1) % array.shape[longest]] + spot[longest + 1:]
    return array.at[tuple(spot)].set(smallest).at[tuple(next_to)].set(largest)


def shard_levels(key, shape, cuts, low, largest):
    def one(dim, parts):
        steps = jax.random.uniform(jax.random.fold_in(jax.random.fold_in(key, 6), dim), (parts,), jnp.float32, low / len(cuts), largest / len(cuts))
        return jnp.repeat(jnp.exp(steps), shape[dim] // parts).reshape((-1,) + (1,) * (len(shape) - dim - 1))

    level = one(*cuts[0])
    for cut in cuts[1:]:
        level = level * one(*cut)
    return level


def noise(own_key, extent, width, most, held_as=jnp.bfloat16):
    drawn = width * jax.random.normal(own_key, extent, jnp.float32)
    return jnp.clip(drawn, min=-most, max=most).astype(held_as)


def setup_inputs(seed: int = 0) -> dict:
    key_list = jax.random.split(jax.random.key(seed), 13)
    offsets = jnp.clip(6.0 * jax.random.uniform(key_list[0], (3, GX, GY, GZ, S), jnp.float32) ** shard_levels(key_list[0], (3, GX, GY, GZ, S), ((1, 4), (2, 8), (3, 16)), -0.2, 0.2), 0.0, 6.0)
    species = touch_ends(jax.random.randint(key_list[1], (GX, GY, GZ, S), 0, NSPEC), jax.random.fold_in(key_list[1], 1), 0, NSPEC - 1).astype(jnp.int32)
    counts = draw_counts(jax.random.fold_in(key_list[12], 71), 0)
    edges = draw_edges(jax.random.fold_in(key_list[12], 71), 0)
    emb = noise(key_list[4], (NSPEC, C), 1.0, 6.0)
    rad_in = noise(key_list[5], (2, NB, RH), NB ** -0.5, 2.0)
    rad_hid = noise(key_list[6], (2, RH, RH), RH ** -0.5, 0.75)
    rad_out = noise(key_list[7], (2, RH, 2 * C), RH ** -0.5, 0.75)
    mix_one = noise(key_list[8], (2, C, C), C ** -0.5, 0.5)
    project = noise(key_list[9], (2, C, C), C ** -0.5, 0.5)
    mix_two = noise(key_list[10], (C, C), C ** -0.5, 0.5)
    readout = noise(key_list[11], (C,), C ** -0.5, 0.5, jnp.float32)
    return dict(offsets=offsets, species=species, counts=counts, edges=edges, emb=emb, rad_in=rad_in, rad_hid=rad_hid, rad_out=rad_out, mix_one=mix_one, project=project, mix_two=mix_two, readout=readout)


cell_length = 6.0

def radial(relative, w_in, w_hid, w_out):
    squared = lax.optimization_barrier(jnp.sum(relative * relative, axis=1, keepdims=True))
    basis_count = w_in.shape[0]
    inverse_widths = 0.1 * 30.0 ** (jnp.arange(basis_count, dtype=jnp.float32) / (basis_count - 1))
    basis_values = jnp.exp(-squared * inverse_widths[None, :]).astype(jnp.bfloat16)
    hidden = jax.nn.silu(jnp.dot(basis_values, w_in, preferred_element_type=jnp.float32)).astype(jnp.bfloat16)
    hidden = jax.nn.silu(jnp.dot(hidden, w_hid, preferred_element_type=jnp.float32)).astype(jnp.bfloat16)
    return jnp.dot(hidden, w_out, preferred_element_type=jnp.float32)

def messages_one(relative, source_rows, radial_out, channels):
    scalar_part = radial_out[:, :channels] * source_rows
    vector_part = radial_out[:, channels:] * source_rows
    return jnp.concatenate([scalar_part, vector_part * relative[:, 0:1], vector_part * relative[:, 1:2], vector_part * relative[:, 2:3]], axis=1)

def messages_two(relative, source_rows, radial_out, channels):
    inner_sum = relative[:, 0:1] * source_rows[:, channels:2 * channels] + relative[:, 1:2] * source_rows[:, 2 * channels:3 * channels] + relative[:, 2:3] * source_rows[:, 3 * channels:]
    return radial_out[:, :channels] * source_rows[:, :channels] + radial_out[:, channels:] * inner_sum

def embedding(species_ids, emb):
    onehot = (species_ids[:, None] == jnp.arange(emb.shape[0], dtype=jnp.int32)[None, :]).astype(jnp.bfloat16)
    return jnp.dot(onehot, emb, preferred_element_type=jnp.float32)

def node_one(summed, mix_one, channels):
    scaled = (summed / DEG ** 0.5).astype(jnp.bfloat16)
    scalars = jax.nn.silu(jnp.dot(scaled[:, :channels], mix_one[0], preferred_element_type=jnp.float32))
    vectors = jnp.dot(scaled[:, channels:].reshape(-1, channels), mix_one[1], preferred_element_type=jnp.float32).reshape(scaled.shape[0], 3 * channels)
    return (scalars, vectors)

def project_up(features, project, channels):
    scalars = jnp.dot(features[:, :channels], project[0], preferred_element_type=jnp.float32)
    vectors = jnp.dot(features[:, channels:].reshape(-1, channels), project[1], preferred_element_type=jnp.float32).reshape(features.shape[0], 3 * channels)
    return jnp.concatenate([scalars, vectors], axis=1).astype(jnp.bfloat16)

def project_back(grads, project, channels):
    scalars = jnp.dot(grads[:, :channels], project[0].astype(jnp.float32).T, precision=lax.Precision.HIGHEST)
    vectors = jnp.dot(grads[:, channels:].reshape(-1, channels), project[1].astype(jnp.float32).T, precision=lax.Precision.HIGHEST).reshape(grads.shape[0], 3 * channels)
    return jnp.concatenate([scalars, vectors], axis=1)

def node_two(summed, scalars, mix_two, readout, occupied):
    scaled = (summed / DEG ** 0.5).astype(jnp.bfloat16)
    mixed_rows = jnp.dot(scaled, mix_two, preferred_element_type=jnp.float32) + scalars
    per_atom = jnp.dot(jax.nn.silu(mixed_rows), readout, precision=lax.Precision.HIGHEST)
    return jnp.sum(per_atom * occupied)

def reference(offsets, species, counts, edges, emb, rad_in, rad_hid, rad_out, mix_one, project, mix_two, readout):
    channels = emb.shape[1]
    own_count = KX * KY * KZ * S
    devices_all = N_GX * N_GY * N_GZ
    atom_count = GX * GY * GZ * S
    positions = offsets.reshape(3, -1).T
    species_all = species.reshape(-1)
    occupied = (jnp.arange(S, dtype=jnp.int32)[None, None, None, :] < counts[..., None]).reshape(-1).astype(jnp.float32)
    grid_shape = (N_GX, N_GY, N_GZ, E_DEV)
    device_x = lax.broadcasted_iota(jnp.int32, grid_shape, 0)
    device_y = lax.broadcasted_iota(jnp.int32, grid_shape, 1)
    device_z = lax.broadcasted_iota(jnp.int32, grid_shape, 2)
    raw_target = edges[0]
    valid_edge = (raw_target >= 0).astype(jnp.float32)
    target = jnp.maximum(raw_target, 0).astype(jnp.int32)
    source = jnp.maximum(edges[1], 0).astype(jnp.int32)
    slot_target = target % S
    cell_target = target // S
    target_z = cell_target % KZ
    target_y = cell_target // KZ % KY
    target_x = cell_target // (KZ * KY)
    slot_source = source % S
    cell_source = source // S
    padded_z = cell_source % (KZ + 2)
    padded_y = cell_source // (KZ + 2) % (KY + 2)
    padded_x = cell_source // ((KZ + 2) * (KY + 2))
    global_x = device_x * KX + target_x
    global_y = device_y * KY + target_y
    global_z = device_z * KZ + target_z
    target_global = (((global_x * GY + global_y) * GZ + global_z) * S + slot_target).astype(jnp.int32)
    source_x = (device_x * KX + padded_x - 1) % GX
    source_y = (device_y * KY + padded_y - 1) % GY
    source_z = (device_z * KZ + padded_z - 1) % GZ
    source_global = (((source_x * GY + source_y) * GZ + source_z) * S + slot_source).astype(jnp.int32)
    cell_shift = jnp.stack([padded_x - 1 - target_x, padded_y - 1 - target_y, padded_z - 1 - target_z], axis=-1).astype(jnp.float32)
    pieces = (target.reshape(devices_all, E_DEV), target_global.reshape(devices_all, E_DEV), source_global.reshape(devices_all, E_DEV), cell_shift.reshape(devices_all, E_DEV, 3), valid_edge.reshape(devices_all, E_DEV))
    table_all = embedding(species_all, emb)

    def gather_terms(which_layer, all_moved, features):

        def device_term(device_data):
            local_target, global_target, global_source, shift_rows, valid_rows = device_data
            relative = shift_rows + (all_moved[global_source] - all_moved[global_target]) / cell_length
            radial_out = radial(relative, rad_in[which_layer], rad_hid[which_layer], rad_out[which_layer])
            if which_layer == 0:
                message = messages_one(relative, features[global_source], radial_out, channels)
            else:
                message = messages_two(relative, features[global_source], radial_out, channels)
            message = message * valid_rows[:, None]
            return jax.ops.segment_sum(message, local_target, own_count)
        stacked = lax.map(jax.checkpoint(device_term), pieces)
        width_out = stacked.shape[-1]
        stacked = stacked.reshape(N_GX, N_GY, N_GZ, KX, KY, KZ, S, width_out)
        return stacked.transpose(0, 3, 1, 4, 2, 5, 6, 7).reshape(atom_count, width_out)
    summed_one, back_one = jax.vjp(lambda all_moved: gather_terms(0, all_moved, table_all), positions)
    (scalars, vectors), back_node_one = jax.vjp(lambda summed: node_one(summed, mix_one, channels), summed_one)
    hidden_state = jnp.concatenate([scalars, vectors], axis=1).astype(jnp.bfloat16)
    lifted = project_up(hidden_state, project, channels).astype(jnp.float32)
    summed_two, back_two = jax.vjp(lambda all_moved, lifted_in: gather_terms(1, all_moved, lifted_in), positions, lifted)
    total_energy, back_node_two = jax.vjp(lambda summed, kept_scalars: node_two(summed, kept_scalars, mix_two, readout, occupied), summed_two, scalars)
    grad_summed, grad_scalars = back_node_two(jnp.ones((), jnp.float32))
    grad_moved_two, grad_lifted = back_two(grad_summed)
    grad_hidden = project_back(grad_lifted, project, channels)
    grad_summed_one, = back_node_one((grad_hidden[:, :channels] + grad_scalars, grad_hidden[:, channels:]))
    grad_moved_one, = back_one(grad_summed_one)
    forces = -(grad_moved_one + grad_moved_two).T.reshape(3, GX, GY, GZ, S)
    energy = total_energy / atom_count
    return (forces, energy)
```

```python
import functools
import itertools

import jax
import jax.numpy as jnp
from jax import lax
from jax.experimental import pallas as pl
from jax.experimental.pallas import tpu as pltpu
from jax.sharding import PartitionSpec as P

F32 = jnp.float32
BF16 = jnp.bfloat16
MESH = pl.DeviceIdType.MESH
AXES = ("gx", "gy", "gz")

C = 128
CELL = 6.0
DEG = 8
ATOMS = 128
EDGES = 1024
WIDTHS = tuple(0.1 * 30.0 ** (k / 7) for k in range(8))
RSQRT = 1.0 / DEG**0.5

NEIGHBOURS = tuple(d for d in itertools.product((-1, 0, 1), repeat=3) if d != (0, 0, 0))
OWN = {-1: slice(1, 2), 0: slice(1, 3), 1: slice(2, 3)}
THERE = {-1: slice(3, 4), 0: slice(1, 3), 1: slice(0, 1)}
HALO = {-1: slice(0, 1), 0: slice(1, 3), 1: slice(3, 4)}


def dot(a, b, ca, cb):
    return lax.dot_general(a, b, (((ca,), (cb,)), ((), ())), preferred_element_type=F32)


def nn(a, b):
    return dot(a, b, 1, 0)


def tn(a, b):
    return dot(a, b, 0, 0)


def nt(a, b):
    return dot(a, b, 1, 1)


def rows_iota(shape):
    return lax.broadcasted_iota(jnp.int32, shape, 0)


def lanes_iota(shape):
    return lax.broadcasted_iota(jnp.int32, shape, 1)


def mask(condition):
    return jnp.where(condition, 1.0, 0.0).astype(BF16)


def fold(x):
    total = x[:, :ATOMS]
    for r in range(1, DEG):
        total = total + x[:, r * ATOMS : (r + 1) * ATOMS]
    return total


def tile(x):
    return jnp.concatenate([x] * DEG, axis=1)


def sigmoid(x):
    return 1.0 / (1.0 + jnp.exp(-x))


def three(x):
    high = x.astype(BF16)
    rest = x - high.astype(F32)
    middle = rest.astype(BF16)
    return high, middle, (rest - middle.astype(F32)).astype(BF16)


def kernel(
    sizes,
    off,
    spe,
    cnt,
    edg,
    emb,
    rin,
    rhid,
    rout,
    mix1,
    proj,
    mix2,
    rdo,
    frc,
    eng,
    geo,
    geo2,
    srt,
    embp,
    ext,
    gt,
    lg,
    dl,
    rad,
    act,
    usrc,
    g32,
    xs,
    xr,
    ys,
    yr,
    zs,
    zr,
    pg,
    pgx,
    pr,
    esx,
    esy,
    esz,
    geo_s,
    geo_r,
    pos_s,
    pos_r,
    ft_s,
    ft_r,
    gr_s,
    gr_r,
    en_s,
    en_r,
):
    me = tuple(lax.axis_index(a) for a in AXES)

    def at(offset):
        return tuple(lax.rem(m + d + n, n) for m, d, n in zip(me, offset, sizes))

    def remote(src, dst, send, recv, offset):
        return pltpu.make_async_remote_copy(
            src_ref=src,
            dst_ref=dst,
            send_sem=send,
            recv_sem=recv,
            device_id=at(offset),
            device_id_type=MESH,
        )

    def axis_offset(axis, d):
        return tuple(d if k == axis else 0 for k in range(3))

    greeted = list(NEIGHBOURS)
    for axis, n in enumerate(sizes):
        greeted += [axis_offset(axis, d) for d in range(2, n - 1)]
    barrier = pltpu.get_barrier_semaphore()
    for d in greeted:
        pl.semaphore_signal(barrier, inc=1, device_id=at(d), device_id_type=MESH)

    for x, y, z in itertools.product(range(2), repeat=3):
        for k in range(3):
            geo[x + 1, y + 1, z + 1, :, k * 16 : k * 16 + 16] = off[k, x, y, z : z + 1, :]
        geo[x + 1, y + 1, z + 1, :, 48:64] = spe[x, y, z : z + 1, :].astype(F32)
        geo[x + 1, y + 1, z + 1, :, 64:128] = jnp.zeros((1, 64), F32)

    pl.semaphore_wait(barrier, len(greeted))
    pending = []
    geo_copies = []
    for i, (dx, dy, dz) in enumerate(NEIGHBOURS):
        copy = remote(
            geo.at[OWN[dx], OWN[dy], OWN[dz]],
            geo.at[THERE[dx], THERE[dy], THERE[dz]],
            geo_s.at[i],
            geo_r.at[i],
            (dx, dy, dz),
        )
        copy.start()
        geo_copies.append(copy)
    pending += geo_copies

    target = edg[0, 0, 0]
    source = edg[1, 0, 0]
    chosen = mask(rows_iota((ATOMS, EDGES)) == target)
    lane2 = lanes_iota((ATOMS, 2 * ATOMS))
    before = mask((rows_iota((ATOMS, 2 * ATOMS)) < lane2) | (lane2 >= ATOMS))
    high_part = (source >> 3).astype(F32)
    low_part = (source & 7).astype(F32)
    base = jnp.zeros((ATOMS, ATOMS), F32)
    table = jnp.zeros((24, ATOMS), F32)
    for b in range(DEG):
        cut = slice(b * ATOMS, (b + 1) * ATOMS)
        part = chosen[:, cut]
        counted = nn(part, before)
        rank = jnp.sum((counted[:, :ATOMS] + base) * part.astype(F32), axis=0, keepdims=True)
        base = base + counted[:, ATOMS:]
        placed = jnp.where(rows_iota((DEG, ATOMS)).astype(F32) == rank, 1.0, 0.0)
        stacked = jnp.concatenate(
            [placed * high_part[:, cut], placed * low_part[:, cut], placed], axis=0
        ).astype(BF16)
        table = table + nt(stacked, part)
    srt[...] = jnp.where(table[16:24] > 0.5, table[0:8] * 8.0 + table[8:16], -1.0).astype(jnp.int32)
    own_lane = lanes_iota((1, ATOMS))
    own_x, own_y, own_z = (own_lane >> 6, (own_lane >> 5) & 1, (own_lane >> 4) & 1)
    own_index = (((own_x + 1) * 4 + own_y + 1) * 4 + own_z + 1) * 16 + (own_lane & 15)
    srow = jnp.concatenate([srt[r : r + 1, :] for r in range(DEG)] + [own_index], axis=1)
    cell = srow >> 4
    slot = srow & 15
    wide = EDGES + ATOMS
    cells = mask(rows_iota((64, wide)) == cell)
    in_slot = (rows_iota((64, wide)) & 15) == slot

    embp[...] = jnp.zeros((ATOMS, C), F32)
    embp[0:89, :] = emb[...].astype(F32)
    pg[...] = jnp.zeros((64, ATOMS), F32)
    widths = jnp.zeros((8, EDGES), F32)
    for k in range(8):
        widths = jnp.where(rows_iota((8, EDGES)) == k, WIDTHS[k], widths)

    for copy in geo_copies:
        copy.wait_recv()
    for i, (x, y, z) in enumerate(itertools.product(range(4), repeat=3)):
        geo2[i : i + 1, :] = geo[x, y, z]
    table_t = geo2[...].T[:64, :]
    got = jnp.zeros((64, wide), F32)
    for part in three(table_t):
        got = got + nn(part, cells)
    got = jnp.where(in_slot, got, 0.0)
    sums = [jnp.sum(got[k * 16 : k * 16 + 16], axis=0, keepdims=True) for k in range(4)]
    near_cell = cell[:, :EDGES]
    steps = (
        (near_cell >> 4) - 1 - tile(own_x),
        ((near_cell >> 2) & 3) - 1 - tile(own_y),
        (near_cell & 3) - 1 - tile(own_z),
    )
    rel = [
        step.astype(F32) + (s[:, :EDGES] - tile(s[:, EDGES:])) / CELL
        for step, s in zip(steps, sums)
    ]
    squared = rel[0] * rel[0] + rel[1] * rel[1] + rel[2] * rel[2]
    basis = jnp.exp(-squared * widths)
    basis_low = basis.astype(BF16)

    def radial(layer):
        first = tn(rin[layer], basis_low)
        gate = sigmoid(first)
        act[layer, 0] = gate * (1.0 + first * (1.0 - gate))
        second = tn(rhid[layer], (first * gate).astype(BF16))
        gate = sigmoid(second)
        act[layer, 1] = gate * (1.0 + second * (1.0 - gate))
        rad[layer] = tn(rout[layer], (second * gate).astype(BF16))

    def radial_back(layer, grad):
        back = nn(rout[layer], grad).astype(BF16).astype(F32) * act[layer, 1]
        back = nn(rhid[layer], back.astype(BF16)).astype(BF16).astype(F32) * act[layer, 0]
        back = nn(rin[layer], back.astype(BF16)).astype(BF16).astype(F32)
        return -2.0 * jnp.sum(back * widths * basis, axis=0, keepdims=True)

    radial(0)
    kinds = jnp.where(srow[:, :EDGES] >= 0, sums[3][:, :EDGES].astype(jnp.int32), -1)
    usrc[...] = tn(embp[...].astype(BF16), mask(rows_iota((ATOMS, EDGES)) == kinds))
    summed = [fold(rad[0, :C] * usrc[...])]
    vector = rad[0, C:] * usrc[...]
    summed += [fold(vector * rel[k]) for k in range(3)]
    scaled = [(s * RSQRT).astype(BF16) for s in summed]
    mixed = tn(mix1[0], scaled[0])
    mixed_gate = sigmoid(mixed)
    scalars = mixed * mixed_gate
    mixed_slope = mixed_gate * (1.0 + mixed * (1.0 - mixed_gate))
    hidden = [scalars.astype(BF16)] + [tn(mix1[1], s).astype(BF16) for s in scaled[1:]]
    for k in range(4):
        lifted = tn(hidden[k], proj[min(k, 1)]).astype(BF16)
        for i, (x, y, z) in enumerate(itertools.product(range(2), repeat=3)):
            ext[x + 1, y + 1, z + 1, :, k * C : (k + 1) * C] = lifted[i * 16 : i * 16 + 16]

    inner, low, high, every = slice(1, 3), slice(0, 1), slice(3, 4), slice(0, 4)
    numbers = itertools.count()

    def pass_on(axis, direction, others):
        i = next(numbers)
        src, dst = list(others), list(others)
        src.insert(axis, OWN[direction])
        dst.insert(axis, THERE[direction])
        copy = remote(
            ext.at[tuple(src)],
            ext.at[tuple(dst)],
            ft_s.at[i],
            ft_r.at[i],
            axis_offset(axis, direction),
        )
        copy.start()
        pending.append(copy)
        return copy

    both = (-1, 1)
    z_copies = [pass_on(2, d, (inner, inner)) for d in both]
    y_copies = [pass_on(1, d, (inner, inner)) for d in both]
    x_copies = [pass_on(0, d, (inner, inner)) for d in both]
    radial(1)
    for copy, rim in zip(z_copies, (high, low)):
        copy.wait_recv()
        y_copies += [pass_on(1, d, (inner, rim)) for d in both]
        x_copies += [pass_on(0, d, (inner, rim)) for d in both]
    for r in range(DEG):
        cut = slice(r * ATOMS, (r + 1) * ATOMS)
        gt[:, cut] = mask(rows_iota((1024, ATOMS)) == srow[:, cut])
    for copy in y_copies:
        copy.wait_recv()
    for rim in (high, low):
        x_copies += [pass_on(0, d, (rim, every)) for d in both]
    readout = jnp.broadcast_to(rdo[...].reshape(1, C), (C, C)).T
    occupied = jnp.zeros((1, ATOMS), F32)
    for i, (x, y, z) in enumerate(itertools.product(range(2), repeat=3)):
        here = ((own_lane >> 4) == i) & ((own_lane & 15) < cnt[x, y, z])
        occupied = jnp.where(here, 1.0, occupied)
    weight = readout * occupied
    for copy in x_copies:
        copy.wait_recv()

    lg[...] = tn(ext[...].reshape(1024, 4 * C), gt[...])
    inner_sum = rel[0] * lg[C : 2 * C] + rel[1] * lg[2 * C : 3 * C] + rel[2] * lg[3 * C :]
    summed_two = fold(rad[1, :C] * lg[:C] + rad[1, C:] * inner_sum)
    rows = tn(mix2[...], (summed_two * RSQRT).astype(BF16)) + scalars
    gate = sigmoid(rows)
    local = jnp.sum(rows * gate * weight, axis=0, keepdims=True)
    local = jnp.sum(local, axis=1, keepdims=True)
    grad_rows = weight * gate * (1.0 + rows * (1.0 - gate))
    grad = tile(nn(mix2[...], grad_rows.astype(BF16)).astype(BF16).astype(F32) * RSQRT)

    def share(axis, buffer, value, first):
        buffer[me[axis]] = jnp.broadcast_to(value, (1, ATOMS))
        copies = []
        for d in range(1, sizes[axis]):
            here = buffer.at[me[axis]]
            copy = remote(
                here, here, en_s.at[first + d - 1], en_r.at[first + d - 1], axis_offset(axis, d)
            )
            copy.start()
            copies.append(copy)
        pending.extend(copies)
        return copies

    def gathered(axis, buffer, copies):
        for copy in copies:
            copy.wait_recv()
        total = buffer[0]
        for i in range(1, sizes[axis]):
            total = total + buffer[i]
        return total[:, 0:1]

    e_copies = share(0, esx, local, 0)

    grad_inner = grad * rad[1, C:]
    dl[:C] = (grad * rad[1, :C]).astype(BF16)
    for k in range(3):
        dl[(k + 1) * C : (k + 2) * C] = (grad_inner * rel[k]).astype(BF16)

    def grad_copy(i, src, dst, axis, direction):
        copy = remote(src, dst, gr_s.at[i], gr_r.at[i], axis_offset(axis, direction))
        copy.start()
        pending.append(copy)
        return copy

    gx_copies = []
    for i, (slab, d) in enumerate(((0, -1), (3, 1))):
        part = nt(gt[slab * 256 : (slab + 1) * 256, :], dl[...]).astype(BF16)
        xs[i] = part.reshape(4, 4, 16, 4 * C)
        gx_copies.append(grad_copy(i, xs.at[i], xr.at[i], 0, d))
    g32[...] = nt(gt[256:768, :], dl[...]).reshape(2, 4, 4, 16, 4 * C)
    direct = [
        jnp.sum(grad_inner * lg[(k + 1) * C : (k + 2) * C], axis=0, keepdims=True)
        for k in range(3)
    ]
    pull = radial_back(
        1, jnp.concatenate([grad * lg[:C], grad * inner_sum], axis=0).astype(BF16)
    )
    drel = [rel[k] * pull + direct[k] for k in range(3)]

    for i, copy in enumerate(gx_copies):
        copy.wait_recv()
        g32[1 - i] = g32[1 - i] + xr[i].astype(F32)
    gy_copies = []
    for i, (rim, d) in enumerate(((0, -1), (3, 1))):
        ys[i] = g32[:, rim].astype(BF16)
        gy_copies.append(grad_copy(2 + i, ys.at[i], yr.at[i], 1, d))
    e_copies = share(1, esy, gathered(0, esx, e_copies), sizes[0])
    for i, copy in enumerate(gy_copies):
        copy.wait_recv()
        g32[:, 2 - i] = g32[:, 2 - i] + yr[i].astype(F32)
    gz_copies = []
    for i, (rim, d) in enumerate(((0, -1), (3, 1))):
        zs[i] = g32[:, 1:3, rim].astype(BF16)
        gz_copies.append(grad_copy(4 + i, zs.at[i], zr.at[i], 2, d))
    e_copies = share(2, esz, gathered(1, esy, e_copies), sizes[0] + sizes[1])
    for i, copy in enumerate(gz_copies):
        copy.wait_recv()
        g32[:, 1:3, 2 - i] = g32[:, 1:3, 2 - i] + zr[i].astype(F32)

    arrived = g32[:, 1:3, 1:3].reshape(ATOMS, 4 * C)

    def project_back(k):
        block = arrived[:, k * C : (k + 1) * C]
        top = block.astype(BF16)
        rest = (block - top.astype(F32)).astype(BF16)
        weights = proj[min(k, 1)]
        return nt(weights, top) + nt(weights, rest)

    grad_mixed = (project_back(0) + grad_rows) * mixed_slope
    grads = [nn(mix1[0], grad_mixed.astype(BF16))]
    grads += [nn(mix1[1], project_back(k).astype(BF16)) for k in range(1, 4)]
    grads = [tile(g.astype(BF16).astype(F32) * RSQRT) for g in grads]

    towards = rel[0] * grads[1] + rel[1] * grads[2] + rel[2] * grads[3]
    pull = radial_back(
        0, jnp.concatenate([grads[0] * usrc[...], towards * usrc[...]], axis=0).astype(BF16)
    )
    vector = rad[0, C:] * usrc[...]
    drel = [
        drel[k] + rel[k] * pull + jnp.sum(vector * grads[k + 1], axis=0, keepdims=True)
        for k in range(3)
    ]

    moved = []
    for k in range(3):
        here = drel[k] / CELL
        both_ends = jnp.concatenate([here, -fold(here)], axis=1)
        moved.append(jnp.broadcast_to(both_ends, (16, wide)))
    moved.append(jnp.zeros((16, wide), F32))
    spread = jnp.where(in_slot, jnp.concatenate(moved, axis=0), 0.0)
    near = jnp.zeros((64, 64), F32)
    for part in three(spread):
        near = near + nt(cells, part)
    pg[:, 0:64] = near
    for i, (x, y, z) in enumerate(itertools.product(range(4), repeat=3)):
        pgx[x, y, z] = pg[i : i + 1, :]
    pos_copies = []
    for i, (dx, dy, dz) in enumerate(NEIGHBOURS):
        copy = remote(
            pgx.at[HALO[dx], HALO[dy], HALO[dz]],
            pr.at[i, 0 : 2 - abs(dx), 0 : 2 - abs(dy), 0 : 2 - abs(dz)],
            pos_s.at[i],
            pos_r.at[i],
            (dx, dy, dz),
        )
        copy.start()
        pos_copies.append(copy)
    pending += pos_copies
    eng[...] = gathered(2, esz, e_copies) / float(ATOMS * sizes[0] * sizes[1] * sizes[2])
    for copy in pos_copies:
        copy.wait_recv()
    for own in itertools.product(range(2), repeat=3):
        total = pgx[own[0] + 1, own[1] + 1, own[2] + 1]
        for i, d in enumerate(NEIGHBOURS):
            if all(s == 0 or (s == -1) == (o == 1) for s, o in zip(d, own)):
                place = tuple(o if s == 0 else 0 for s, o in zip(d, own))
                total = total + pr[(i,) + place]
        for k in range(3):
            frc[k, own[0], own[1], own[2] : own[2] + 1, :] = -total[:, k * 16 : k * 16 + 16]
    for copy in pending:
        copy.wait_send()


def body(sizes, *args):
    vmem = pl.BlockSpec(memory_space=pltpu.VMEM)
    specs = [vmem] * len(args)
    specs[2] = pl.BlockSpec(memory_space=pltpu.SMEM)
    energy_sends = sum(sizes)
    dma = pltpu.SemaphoreType.DMA
    scratch = [
        pltpu.VMEM((4, 4, 4, 1, 128), F32),
        pltpu.VMEM((64, 128), F32),
        pltpu.VMEM((8, 128), jnp.int32),
        pltpu.VMEM((128, 128), F32),
        pltpu.VMEM((4, 4, 4, 16, 512), BF16),
        pltpu.VMEM((1024, 1024), BF16),
        pltpu.VMEM((512, 1024), F32),
        pltpu.VMEM((512, 1024), BF16),
        pltpu.VMEM((2, 256, 1024), F32),
        pltpu.VMEM((2, 2, 64, 1024), F32),
        pltpu.VMEM((128, 1024), F32),
        pltpu.VMEM((2, 4, 4, 16, 512), F32),
        pltpu.VMEM((2, 4, 4, 16, 512), BF16),
        pltpu.VMEM((2, 4, 4, 16, 512), BF16),
        pltpu.VMEM((2, 2, 4, 16, 512), BF16),
        pltpu.VMEM((2, 2, 4, 16, 512), BF16),
        pltpu.VMEM((2, 2, 2, 16, 512), BF16),
        pltpu.VMEM((2, 2, 2, 16, 512), BF16),
        pltpu.VMEM((64, 128), F32),
        pltpu.VMEM((4, 4, 4, 1, 128), F32),
        pltpu.VMEM((26, 2, 2, 2, 1, 128), F32),
        pltpu.VMEM((sizes[0], 1, 128), F32),
        pltpu.VMEM((sizes[1], 1, 128), F32),
        pltpu.VMEM((sizes[2], 1, 128), F32),
        dma((26,)),
        dma((26,)),
        dma((26,)),
        dma((26,)),
        dma((18,)),
        dma((18,)),
        dma((6,)),
        dma((6,)),
        dma((energy_sends,)),
        dma((energy_sends,)),
    ]
    forces, energy = pl.pallas_call(
        functools.partial(kernel, sizes),
        out_shape=(
            jax.ShapeDtypeStruct(args[0].shape, F32),
            jax.ShapeDtypeStruct((1, 1), F32),
        ),
        in_specs=specs,
        out_specs=(vmem, vmem),
        scratch_shapes=scratch,
        compiler_params=pltpu.CompilerParams(
            collective_id=0, has_side_effects=True, vmem_limit_bytes=48 * 1024 * 1024
        ),
    )(*args)
    return forces, energy.reshape(())


def solution(mesh):
    sizes = tuple(mesh.shape[a] for a in AXES)
    in_specs = (
        P(None, "gx", "gy", "gz", None),
        P("gx", "gy", "gz", None),
        P("gx", "gy", "gz"),
        P(None, "gx", "gy", "gz", None),
    ) + (P(),) * 8
    out_specs = (P(None, "gx", "gy", "gz", None), P())
    return jax.shard_map(
        functools.partial(body, sizes),
        mesh=mesh,
        in_specs=in_specs,
        out_specs=out_specs,
        check_vma=False,
    )
```

```python
import functools
import itertools

import jax
import jax.numpy as jnp
from jax import lax
from jax.experimental import pallas as pl
from jax.experimental.pallas import tpu as pltpu
from jax.sharding import PartitionSpec as P

F32 = jnp.float32
BF16 = jnp.bfloat16
MESH = pl.DeviceIdType.MESH
AXES = ("gx", "gy", "gz")

C = 128
CELL = 6.0
DEG = 8
ATOMS = 128
EDGES = 1024
WIDTHS = tuple(0.1 * 30.0 ** (k / 7) for k in range(8))
RSQRT = 1.0 / DEG**0.5

NEIGHBOURS = tuple(d for d in itertools.product((-1, 0, 1), repeat=3) if d != (0, 0, 0))
OWN_CELLS = tuple(itertools.product(range(2), repeat=3))
CHUNKS = 8


def place(d):
    return ((d[0] + 1) * 3 + d[1] + 1) * 3 + d[2] + 1


def chunk_of(d):
    return abs(d[0]) * 4 + abs(d[1]) * 2 + abs(d[2])


def dot(a, b, ca, cb):
    return lax.dot_general(a, b, (((ca,), (cb,)), ((), ())), preferred_element_type=F32)


def nn(a, b):
    return dot(a, b, 1, 0)


def tn(a, b):
    return dot(a, b, 0, 0)


def nt(a, b):
    return dot(a, b, 1, 1)


def rows_iota(shape):
    return lax.broadcasted_iota(jnp.int32, shape, 0)


def lanes_iota(shape):
    return lax.broadcasted_iota(jnp.int32, shape, 1)


def mask(condition):
    return jnp.where(condition, 1.0, 0.0).astype(BF16)


def fold(x):
    total = x[:, :ATOMS]
    for r in range(1, DEG):
        total = total + x[:, r * ATOMS : (r + 1) * ATOMS]
    return total


def tile(x):
    return jnp.concatenate([x] * DEG, axis=1)


def silu(x):
    half = 0.5 * x
    up = 1.0 + jnp.tanh(half)
    return half * up, up * (0.5 + half * (1.0 - 0.5 * up))


def two(x):
    high = x.astype(BF16)
    return high, (x - high.astype(F32)).astype(BF16)


def kernel(
    sizes,
    off,
    spe,
    cnt,
    edg,
    emb,
    rin,
    rhid,
    rout,
    mix1,
    proj,
    mix2,
    rdo,
    frc,
    eng,
    vm,
    in_sem,
    blk,
    sel,
    geo,
    srt,
    embp,
    bas,
    rls,
    nqs,
    ohot,
    rad,
    rad2,
    act,
    act2,
    usrc,
    scl,
    gt,
    lg,
    dl,
    gsum,
    drs,
    tgs,
    pgs,
    pgx,
    pr,
    esx,
    esy,
    esz,
    geo_s,
    geo_r,
    pos_s,
    pos_r,
    en_s,
    en_r,
):
    me = tuple(lax.axis_index(a) for a in AXES)
    incoming = (off, spe, cnt, edg, emb, rin, rhid, rout, mix1, proj, mix2, rdo)
    loads = []
    for i, (src, dst) in enumerate(zip(incoming, vm)):
        loads.append(pltpu.make_async_copy(src, dst, in_sem.at[i]))
    for i in (3, 0, 1, 2, 4, 5, 6, 7, 8, 9, 10, 11):
        loads[i].start()
    off, spe, cnt, edg, emb, rin, rhid, rout, mix1, proj, mix2, rdo = vm

    def at(offset):
        return tuple(lax.rem(m + d + n, n) for m, d, n in zip(me, offset, sizes))

    def remote(src, dst, send, recv, offset):
        return pltpu.make_async_remote_copy(
            src_ref=src,
            dst_ref=dst,
            send_sem=send,
            recv_sem=recv,
            device_id=at(offset),
            device_id_type=MESH,
        )

    def axis_offset(axis, d):
        return tuple(d if k == axis else 0 for k in range(3))

    greeted = list(NEIGHBOURS)
    for axis, n in enumerate(sizes):
        greeted += [axis_offset(axis, d) for d in range(2, n - 1)]
    barrier = pltpu.get_barrier_semaphore()
    for d in greeted:
        pl.semaphore_signal(barrier, inc=1, device_id=at(d), device_id_type=MESH)

    loads[3].wait()
    target = edg[0, 0, 0]
    source = edg[1, 0, 0]
    chosen = mask(rows_iota((ATOMS, EDGES)) == target)
    lane2 = lanes_iota((ATOMS, 2 * ATOMS))
    before = mask((rows_iota((ATOMS, 2 * ATOMS)) < lane2) | (lane2 >= ATOMS))
    high_part = (source >> 3).astype(F32)
    low_part = (source & 7).astype(F32)
    base = jnp.zeros((ATOMS, ATOMS), F32)
    table = jnp.zeros((24, ATOMS), F32)
    for b in range(DEG):
        cut = slice(b * ATOMS, (b + 1) * ATOMS)
        part = chosen[:, cut]
        counted = nn(part, before)
        rank = jnp.sum((counted[:, :ATOMS] + base) * part.astype(F32), axis=0, keepdims=True)
        base = base + counted[:, ATOMS:]
        placed = jnp.where(rows_iota((DEG, ATOMS)).astype(F32) == rank, 1.0, 0.0)
        stacked = jnp.concatenate(
            [placed * high_part[:, cut], placed * low_part[:, cut], placed], axis=0
        ).astype(BF16)
        table = table + nt(stacked, part)
    found = table[0:8] * 8.0 + table[8:16] + table[16:24]
    mine = place((0, 0, 0))
    blk[mine, 0:4, :] = found[0:4] * 2048.0 + found[4:8]

    loads[0].wait()
    loads[1].wait()
    for i, (x, y, z) in enumerate(OWN_CELLS):
        here = slice(i * 16, i * 16 + 16)
        for k in range(3):
            blk[mine, 4 + k : 5 + k, here] = off[k, x, y, z : z + 1, :]
        blk[mine, 7:8, here] = spe[x, y, z : z + 1, :].astype(F32)

    pl.semaphore_wait(barrier, len(greeted))
    pending = []
    geo_copies = []
    for i, d in enumerate(NEIGHBOURS):
        there = place(tuple(-k for k in d))
        copy = remote(blk.at[mine], blk.at[there], geo_s.at[i], geo_r.at[i], d)
        copy.start()
        geo_copies.append(copy)
    pending += geo_copies

    for i in (2, 4, 5, 6, 7, 8, 9, 10, 11):
        loads[i].wait()
    embp[...] = jnp.zeros((ATOMS, C), F32)
    embp[0:89, :] = emb[...].astype(F32)
    geo[...] = jnp.zeros((112, ATOMS), F32)
    drs[...] = jnp.zeros((CHUNKS, 8, EDGES), F32)
    widths = jnp.zeros((8, EDGES), F32)
    for k in range(8):
        widths = jnp.where(rows_iota((8, EDGES)) == k, WIDTHS[k], widths)
    own_lane = lanes_iota((1, ATOMS))
    own_cell = (own_lane >> 6, (own_lane >> 5) & 1, (own_lane >> 4) & 1)
    readout = jnp.broadcast_to(rdo[...].reshape(1, C), (C, C)).T
    occupied = jnp.zeros((1, ATOMS), F32)
    for i, (x, y, z) in enumerate(OWN_CELLS):
        here = ((own_lane >> 4) == i) & ((own_lane & 15) < cnt[x, y, z])
        occupied = jnp.where(here, 1.0, occupied)
    weight = readout * occupied

    def lanes_of(d):
        chosen = own_lane >= 0
        for step, cell in zip(d, own_cell):
            if step:
                chosen = chosen & (cell == (0 if step > 0 else 1))
        return chosen

    for copy in geo_copies:
        copy.wait_recv()
    gathered_blocks = [jnp.zeros((8, ATOMS), F32)] * CHUNKS
    for d in itertools.product((-1, 0, 1), repeat=3):
        n = place(d)
        block = blk[n]
        geo[n * 4 : n * 4 + 4, :] = block[4:8]
        a = chunk_of(d)
        gathered_blocks[a] = jnp.where(lanes_of(d), block, gathered_blocks[a])
    for a in range(CHUNKS):
        sel[a] = gathered_blocks[a]
        packed = gathered_blocks[a][0:4].astype(jnp.int32)
        srt[a] = jnp.concatenate([packed >> 11, packed & 2047], axis=0) - 1
    places = two(geo[...])

    def radial(weights, basis_low, act, out):
        first, slope = silu(tn(rin[weights], basis_low))
        act[0] = slope
        second, slope = silu(tn(rhid[weights], first.astype(BF16)))
        act[1] = slope
        out[...] = tn(rout[weights], second.astype(BF16))

    def radial_back(weights, grad, basis, act):
        back = nn(rout[weights], grad) * act[1]
        back = nn(rhid[weights], back.astype(BF16)) * act[0]
        back = nn(rin[weights], back.astype(BF16))
        return -2.0 * jnp.sum(back * widths * basis, axis=0, keepdims=True)

    def forward(a, carry):
        far = ((a >> 2) & 1, (a >> 1) & 1, a & 1)
        srow = jnp.concatenate([srt[a, r : r + 1, :] for r in range(DEG)], axis=1)
        cell = srow >> 4
        near = (cell >> 4, (cell >> 2) & 3, cell & 3)
        cells = [(p + 1) & 1 for p in near]
        atom = ((cells[0] * 2 + cells[1]) * 2 + cells[2]) * 16 + (srow & 15)
        device = jnp.zeros((1, EDGES), jnp.int32)
        for p, f, own in zip(near, far, own_cell):
            device = device * 3 + ((p + 1) >> 1) + tile(f * (1 - 2 * own))
        device = jnp.where(srow >= 0, device, -1)
        nqs[a] = device
        onehot = mask(rows_iota((ATOMS, EDGES)) == atom)
        ohot[a] = onehot
        found = nn(places[0], onehot) + nn(places[1], onehot)
        found = jnp.where((rows_iota((112, EDGES)) >> 2) == device, found, 0.0)
        total = found[0:8]
        for i in range(1, 14):
            total = total + found[i * 8 : i * 8 + 8]
        total = total[0:4] + total[4:8]
        rel = []
        for k in range(3):
            step = (near[k] - 1 - tile(own_cell[k])).astype(F32)
            rel.append(step + (total[k : k + 1] - tile(sel[a, 4 + k : 5 + k, :])) / CELL)
            rls[a, k : k + 1, :] = rel[k]
        squared = rel[0] * rel[0] + rel[1] * rel[1] + rel[2] * rel[2]
        basis = jnp.exp(-squared * widths)
        bas[a] = basis
        radial(0, basis.astype(BF16), act.at[a], rad.at[a])
        kinds = jnp.where(srow >= 0, total[3:4].astype(jnp.int32), -1)
        kept = tn(embp[...].astype(BF16), mask(rows_iota((ATOMS, EDGES)) == kinds))
        usrc[a] = kept
        where = pl.ds(pl.multiple_of(a * ATOMS, ATOMS), ATOMS)
        scl[0:C, where] = (fold(rad[a, :C] * kept) * RSQRT).astype(BF16)
        vector = rad[a, C:] * kept
        for k in range(3):
            scl[(k + 1) * C : (k + 2) * C, where] = (fold(vector * rel[k]) * RSQRT).astype(BF16)
        return carry

    lax.fori_loop(0, CHUNKS, forward, 0)

    scalars, mixed_slope = silu(tn(mix1[0], scl[:C]))
    hidden = [scalars.astype(BF16)]
    hidden += [tn(mix1[1], scl[k * C : (k + 1) * C]).astype(BF16) for k in range(1, 4)]
    lifted = [tn(proj[min(k, 1)], hidden[k]).astype(BF16) for k in range(4)]

    srow = jnp.concatenate([srt[0, r : r + 1, :] for r in range(DEG)], axis=1)
    cell = srow >> 4
    near = (cell >> 4, (cell >> 2) & 3, cell & 3)
    chunk = jnp.zeros((1, EDGES), jnp.int32)
    atom = jnp.zeros((1, EDGES), jnp.int32)
    for p in near:
        chunk = chunk * 2 + 1 - (((p + 1) >> 1) & 1)
        atom = atom * 2 + ((p + 1) & 1)
    row = jnp.where(srow >= 0, chunk * ATOMS + atom * 16 + (srow & 15), -1)
    gt[...] = mask(rows_iota((1024, EDGES)) == row)
    radial(1, bas[0].astype(BF16), act2, rad2)
    rel = [rls[0, k : k + 1, :] for k in range(3)]
    for k in range(4):
        lg[k * C : (k + 1) * C, :] = nn(lifted[k], gt[...])
    inner_sum = rel[0] * lg[C : 2 * C] + rel[1] * lg[2 * C : 3 * C] + rel[2] * lg[3 * C :]
    summed_two = fold(rad2[:C] * lg[:C] + rad2[C:] * inner_sum)
    rows = tn(mix2[...], (summed_two * RSQRT).astype(BF16)) + scalars[:, :ATOMS]
    energy, slope = silu(rows)
    local = jnp.sum(energy * weight, axis=0, keepdims=True)
    local = jnp.sum(local, axis=1, keepdims=True)
    grad_rows = weight * slope
    grad = tile(nn(mix2[...], grad_rows.astype(BF16)) * RSQRT)

    def share(axis, buffer, value, first):
        buffer[me[axis]] = jnp.broadcast_to(value, (1, ATOMS))
        copies = []
        for d in range(1, sizes[axis]):
            here = buffer.at[me[axis]]
            copy = remote(
                here, here, en_s.at[first + d - 1], en_r.at[first + d - 1], axis_offset(axis, d)
            )
            copy.start()
            copies.append(copy)
        pending.extend(copies)
        return copies

    def gathered(axis, buffer, copies):
        for copy in copies:
            copy.wait_recv()
        total = buffer[0]
        for i in range(1, sizes[axis]):
            total = total + buffer[i]
        return total[:, 0:1]

    e_copies = share(0, esx, local, 0)

    grad_inner = grad * rad2[C:]
    dl[:C] = (grad * rad2[:C]).astype(BF16)
    for k in range(3):
        dl[(k + 1) * C : (k + 2) * C] = (grad_inner * rel[k]).astype(BF16)
    back = [nt(dl[k * C : (k + 1) * C], gt[...]) for k in range(4)]
    pull = radial_back(
        1,
        jnp.concatenate([grad * lg[:C], grad * inner_sum], axis=0).astype(BF16),
        bas[0],
        act2,
    )
    for k in range(3):
        direct = jnp.sum(grad_inner * lg[(k + 1) * C : (k + 2) * C], axis=0, keepdims=True)
        drs[0, k : k + 1, :] = rel[k] * pull + direct

    e_copies = share(1, esy, gathered(0, esx, e_copies), sizes[0])
    back = [nn(proj[min(k, 1)], back[k].astype(BF16)) for k in range(4)]
    own_rows = jnp.concatenate([grad_rows, jnp.zeros((C, 1024 - ATOMS), F32)], axis=1)
    back[0] = (back[0] + own_rows) * mixed_slope
    for k in range(4):
        gsum[k * C : (k + 1) * C] = nn(mix1[min(k, 1)], back[k].astype(BF16)) * RSQRT
    pgs[...] = jnp.zeros((112, ATOMS), F32)

    def backward(a, carry):
        where = pl.ds(pl.multiple_of(a * ATOMS, ATOMS), ATOMS)
        grads = [tile(gsum[k * C : (k + 1) * C, where]) for k in range(4)]
        rel = [rls[a, k : k + 1, :] for k in range(3)]
        towards = rel[0] * grads[1] + rel[1] * grads[2] + rel[2] * grads[3]
        kept = usrc[a]
        pull = radial_back(
            0,
            jnp.concatenate([grads[0] * kept, towards * kept], axis=0).astype(BF16),
            bas[a],
            act.at[a],
        )
        vector = rad[a, C:] * kept
        moved = []
        for k in range(3):
            direct = jnp.sum(vector * grads[k + 1], axis=0, keepdims=True)
            moved.append((drs[a, k : k + 1, :] + rel[k] * pull + direct) / CELL)
            tgs[a, k : k + 1, :] = fold(moved[k])
        moved.append(jnp.zeros((1, EDGES), F32))
        moved = jnp.concatenate(moved + moved, axis=0)
        spread = jnp.concatenate([moved] * 14, axis=0)
        spread = jnp.where((rows_iota((112, EDGES)) >> 2) == nqs[a], spread, 0.0)
        onehot = ohot[a]
        top, rest = two(spread)
        pgs[...] += nt(top, onehot) + nt(rest, onehot)
        return carry

    tgs[...] = jnp.zeros((CHUNKS, 4, ATOMS), F32)
    lax.fori_loop(0, 1, backward, 0)
    e_copies = share(2, esz, gathered(1, esy, e_copies), sizes[0] + sizes[1])
    lax.fori_loop(1, CHUNKS, backward, 0)

    pos_copies = []
    for d in itertools.product((-1, 0, 1), repeat=3):
        n = place(d)
        pgx[n] = pgs[n * 4 : n * 4 + 4, :] - jnp.where(lanes_of(d), tgs[chunk_of(d)], 0.0)
    for i, d in enumerate(NEIGHBOURS):
        there = place(tuple(-k for k in d))
        copy = remote(pgx.at[place(d)], pr.at[there], pos_s.at[i], pos_r.at[i], d)
        copy.start()
        pos_copies.append(copy)
    pending += pos_copies
    eng[...] = gathered(2, esz, e_copies) / float(ATOMS * sizes[0] * sizes[1] * sizes[2])
    for copy in pos_copies:
        copy.wait_recv()
    total = pgx[mine]
    for d in NEIGHBOURS:
        total = total + pr[place(d)]
    for i, (x, y, z) in enumerate(OWN_CELLS):
        for k in range(3):
            frc[k, x, y, z : z + 1, :] = -total[k : k + 1, i * 16 : i * 16 + 16]
    for copy in pending:
        copy.wait_send()


def body(sizes, *args):
    hbm = pl.BlockSpec(memory_space=pltpu.HBM)
    vmem = pl.BlockSpec(memory_space=pltpu.VMEM)
    held = [pltpu.VMEM(a.shape, a.dtype) for a in args]
    held[2] = pltpu.SMEM(args[2].shape, args[2].dtype)
    energy_sends = sum(sizes)
    dma = pltpu.SemaphoreType.DMA
    scratch = [
        tuple(held),
        dma((len(args),)),
        pltpu.VMEM((27, 8, 128), F32),
        pltpu.VMEM((8, 8, 128), F32),
        pltpu.VMEM((112, 128), F32),
        pltpu.VMEM((8, 8, 128), jnp.int32),
        pltpu.VMEM((128, 128), F32),
        pltpu.VMEM((8, 8, 1024), F32),
        pltpu.VMEM((8, 3, 1024), F32),
        pltpu.VMEM((8, 1, 1024), jnp.int32),
        pltpu.VMEM((8, 128, 1024), BF16),
        pltpu.VMEM((8, 256, 1024), F32),
        pltpu.VMEM((256, 1024), F32),
        pltpu.VMEM((8, 2, 64, 1024), F32),
        pltpu.VMEM((2, 64, 1024), F32),
        pltpu.VMEM((8, 128, 1024), F32),
        pltpu.VMEM((512, 1024), BF16),
        pltpu.VMEM((1024, 1024), BF16),
        pltpu.VMEM((512, 1024), F32),
        pltpu.VMEM((512, 1024), BF16),
        pltpu.VMEM((512, 1024), F32),
        pltpu.VMEM((8, 8, 1024), F32),
        pltpu.VMEM((8, 4, 128), F32),
        pltpu.VMEM((112, 128), F32),
        pltpu.VMEM((27, 4, 128), F32),
        pltpu.VMEM((27, 4, 128), F32),
        pltpu.VMEM((sizes[0], 1, 128), F32),
        pltpu.VMEM((sizes[1], 1, 128), F32),
        pltpu.VMEM((sizes[2], 1, 128), F32),
        dma((26,)),
        dma((26,)),
        dma((26,)),
        dma((26,)),
        dma((energy_sends,)),
        dma((energy_sends,)),
    ]
    forces, energy = pl.pallas_call(
        functools.partial(kernel, sizes),
        out_shape=(
            jax.ShapeDtypeStruct(args[0].shape, F32),
            jax.ShapeDtypeStruct((1, 1), F32),
        ),
        in_specs=[hbm] * len(args),
        out_specs=(vmem, vmem),
        scratch_shapes=scratch,
        compiler_params=pltpu.CompilerParams(
            collective_id=0, has_side_effects=True, vmem_limit_bytes=62 * 1024 * 1024
        ),
    )(*args)
    return forces, energy.reshape(())


def solution(mesh):
    sizes = tuple(mesh.shape[a] for a in AXES)
    in_specs = (
        P(None, "gx", "gy", "gz", None),
        P("gx", "gy", "gz", None),
        P("gx", "gy", "gz"),
        P(None, "gx", "gy", "gz", None),
    ) + (P(),) * 8
    out_specs = (P(None, "gx", "gy", "gz", None), P())
    return jax.shard_map(
        functools.partial(body, sizes),
        mesh=mesh,
        in_specs=in_specs,
        out_specs=out_specs,
        check_vma=False,
    )
```

```python
import functools
import itertools

import jax
import jax.numpy as jnp
from jax import lax
from jax.experimental import pallas as pl
from jax.experimental.pallas import tpu as pltpu
from jax.sharding import PartitionSpec as P

F32 = jnp.float32
BF16 = jnp.bfloat16
MESH = pl.DeviceIdType.MESH
AXES = ("gx", "gy", "gz")

C = 128
CELL = 6.0
DEG = 8
ATOMS = 128
EDGES = 1024
WIDTHS = tuple(0.1 * 30.0 ** (k / 7) for k in range(8))
RSQRT = 1.0 / DEG**0.5

NEIGHBOURS = tuple(
    sorted(
        (d for d in itertools.product((-1, 0, 1), repeat=3) if d != (0, 0, 0)),
        key=lambda d: (-abs(d[2]), -abs(d[0]) - abs(d[1])),
    )
)
OWN_CELLS = tuple(itertools.product(range(2), repeat=3))
CHUNKS = 8
KINDS = 96


def place(d):
    return ((d[0] + 1) * 3 + d[1] + 1) * 3 + d[2] + 1


def chunk_of(d):
    return abs(d[0]) * 4 + abs(d[1]) * 2 + abs(d[2])


def dot(a, b, ca, cb):
    return lax.dot_general(a, b, (((ca,), (cb,)), ((), ())), preferred_element_type=F32)


def nn(a, b):
    return dot(a, b, 1, 0)


def tn(a, b):
    return dot(a, b, 0, 0)


def nt(a, b):
    return dot(a, b, 1, 1)


def rows_iota(shape):
    return lax.broadcasted_iota(jnp.int32, shape, 0)


def lanes_iota(shape):
    return lax.broadcasted_iota(jnp.int32, shape, 1)


def mask(condition):
    return jnp.where(condition, 1.0, 0.0).astype(BF16)


def fold(x):
    total = x[:, :ATOMS]
    for r in range(1, DEG):
        total = total + x[:, r * ATOMS : (r + 1) * ATOMS]
    return total


def tile(x):
    return jnp.concatenate([x] * DEG, axis=1)


def silu_of_half(half):
    up = 1.0 + jnp.tanh(half)
    value = half * up
    gate = 0.5 * up
    return value, gate + value * (1.0 - gate)


def silu(x):
    return silu_of_half(0.5 * x)


def two(x):
    high = x.astype(BF16)
    return high, (x - high.astype(F32)).astype(BF16)


def kernel(
    sizes,
    off,
    spe,
    cnt,
    edg,
    emb,
    rin,
    rhid,
    rout,
    mix1,
    proj,
    mix2,
    rdo,
    frc,
    eng,
    vm,
    in_sem,
    blk,
    sel,
    geo,
    srt,
    embp,
    bas,
    rls,
    nqs,
    ohot,
    vec,
    rad2,
    act,
    act2,
    usrc,
    scl,
    gt,
    gtt,
    lg,
    dl,
    gsum,
    drs,
    tgs,
    pgs,
    pgx,
    pr,
    esx,
    esy,
    esz,
    geo_s,
    geo_r,
    pos_s,
    pos_r,
    en_s,
    en_r,
):
    me = tuple(lax.axis_index(a) for a in AXES)
    incoming = (off, spe, cnt, edg, emb, rin, rhid, rout, mix1, proj, mix2, rdo)
    loads = []
    for i, (src, dst) in enumerate(zip(incoming, vm)):
        loads.append(pltpu.make_async_copy(src, dst, in_sem.at[i]))
    for i in (3, 0, 1, 2, 4, 5, 6, 7, 8, 9, 10, 11):
        loads[i].start()
    off, spe, cnt, edg, emb, rin, rhid, rout, mix1, proj, mix2, rdo = vm

    def at(offset):
        return tuple(lax.rem(m + d + n, n) for m, d, n in zip(me, offset, sizes))

    def remote(src, dst, send, recv, offset):
        return pltpu.make_async_remote_copy(
            src_ref=src,
            dst_ref=dst,
            send_sem=send,
            recv_sem=recv,
            device_id=at(offset),
            device_id_type=MESH,
        )

    def axis_offset(axis, d):
        return tuple(d if k == axis else 0 for k in range(3))

    greeted = list(NEIGHBOURS)
    for axis, n in enumerate(sizes):
        greeted += [axis_offset(axis, d) for d in range(2, n - 1)]
    barrier = pltpu.get_barrier_semaphore()
    for d in greeted:
        pl.semaphore_signal(barrier, inc=1, device_id=at(d), device_id_type=MESH)

    loads[3].wait()
    target = edg[0, 0, 0]
    source = edg[1, 0, 0]
    chosen = mask(rows_iota((ATOMS, EDGES)) == target)
    lane2 = lanes_iota((ATOMS, 2 * ATOMS))
    before = mask((rows_iota((ATOMS, 2 * ATOMS)) < lane2) | (lane2 >= ATOMS))
    high_part = (source >> 3).astype(F32)
    low_part = (source & 7).astype(F32)
    base = jnp.zeros((ATOMS, ATOMS), F32)
    table = jnp.zeros((24, ATOMS), F32)
    for b in range(DEG):
        cut = slice(b * ATOMS, (b + 1) * ATOMS)
        part = chosen[:, cut]
        counted = nn(part, before)
        rank = jnp.sum((counted[:, :ATOMS] + base) * part.astype(F32), axis=0, keepdims=True)
        base = base + counted[:, ATOMS:]
        placed = jnp.where(rows_iota((DEG, ATOMS)).astype(F32) == rank, 1.0, 0.0)
        stacked = jnp.concatenate(
            [placed * high_part[:, cut], placed * low_part[:, cut], placed], axis=0
        ).astype(BF16)
        table = table + nt(stacked, part)
    found = table[0:8] * 8.0 + table[8:16] + table[16:24]
    mine = place((0, 0, 0))
    blk[mine, 0:4, :] = found[0:4] * 2048.0 + found[4:8]

    loads[0].wait()
    loads[1].wait()
    for i, (x, y, z) in enumerate(OWN_CELLS):
        here = slice(i * 16, i * 16 + 16)
        for k in range(3):
            blk[mine, 4 + k : 5 + k, here] = off[k, x, y, z : z + 1, :]
        blk[mine, 7:8, here] = spe[x, y, z : z + 1, :].astype(F32)

    pl.semaphore_wait(barrier, len(greeted))
    pending = []
    geo_copies = []
    for i, d in enumerate(NEIGHBOURS):
        there = place(tuple(-k for k in d))
        copy = remote(blk.at[mine], blk.at[there], geo_s.at[i], geo_r.at[i], d)
        copy.start()
        geo_copies.append(copy)
    pending += geo_copies

    for i in (2, 4, 5, 6, 7, 8, 9, 10, 11):
        loads[i].wait()
    half_in = [(0.5 * rin[k].astype(F32)).astype(BF16) for k in range(2)]
    half_hid = [(0.5 * rhid[k].astype(F32)).astype(BF16) for k in range(2)]
    embp[...] = jnp.zeros((KINDS, C), F32)
    embp[0:89, :] = emb[...].astype(F32)
    geo[...] = jnp.zeros((112, ATOMS), F32)
    widths = jnp.zeros((8, EDGES), F32)
    for k in range(8):
        widths = jnp.where(rows_iota((8, EDGES)) == k, WIDTHS[k], widths)
    own_lane = lanes_iota((1, ATOMS))
    own_cell = (own_lane >> 6, (own_lane >> 5) & 1, (own_lane >> 4) & 1)
    readout = jnp.broadcast_to(rdo[...].reshape(1, C), (C, C)).T
    occupied = jnp.zeros((1, ATOMS), F32)
    for i, (x, y, z) in enumerate(OWN_CELLS):
        here = ((own_lane >> 4) == i) & ((own_lane & 15) < cnt[x, y, z])
        occupied = jnp.where(here, 1.0, occupied)
    weight = readout * occupied

    source_row = found.astype(jnp.int32) - 1
    srt[0] = source_row
    cell = source_row >> 4
    near = (cell >> 4, (cell >> 2) & 3, cell & 3)
    chunk = jnp.zeros((DEG, ATOMS), jnp.int32)
    atom = jnp.zeros((DEG, ATOMS), jnp.int32)
    for p in near:
        chunk = chunk * 2 + 1 - (((p + 1) >> 1) & 1)
        atom = atom * 2 + ((p + 1) & 1)
    row = jnp.where(source_row >= 0, chunk * ATOMS + atom * 16 + (source_row & 15), -1)
    srt[1] = row
    column = row.astype(F32).T
    for r in range(DEG):
        cut = slice(r * ATOMS, (r + 1) * ATOMS)
        gt[:, cut] = mask(rows_iota((1024, ATOMS)) == srt[1, r : r + 1, :])
        at_lane = lanes_iota((ATOMS, 1024)).astype(F32)
        gtt[cut, :] = mask(at_lane == column[:, r : r + 1])

    def lanes_of(d):
        chosen = own_lane >= 0
        for step, cell in zip(d, own_cell):
            if step:
                chosen = chosen & (cell == (0 if step > 0 else 1))
        return chosen

    for copy in geo_copies:
        copy.wait_recv()
    gathered_blocks = [jnp.zeros((8, ATOMS), F32)] * CHUNKS
    for d in itertools.product((-1, 0, 1), repeat=3):
        n = place(d)
        block = blk[n]
        geo[n * 4 : n * 4 + 4, :] = block[4:8]
        a = chunk_of(d)
        gathered_blocks[a] = jnp.where(lanes_of(d), block, gathered_blocks[a])
    for a in range(CHUNKS):
        sel[a] = gathered_blocks[a]
        if a:
            packed = gathered_blocks[a][0:4].astype(jnp.int32)
            srt[a] = jnp.concatenate([packed >> 11, packed & 2047], axis=0) - 1
    places = jnp.concatenate(two(geo[...]), axis=1)

    def radial(weights, basis_low, act):
        first, slope = silu_of_half(tn(half_in[weights], basis_low))
        act[0] = slope
        second, slope = silu_of_half(tn(half_hid[weights], first.astype(BF16)))
        act[1] = slope
        return tn(rout[weights], second.astype(BF16))

    def radial_back(weights, grad, basis, act):
        back = nn(rout[weights], grad) * act[1]
        back = nn(rhid[weights], back.astype(BF16)) * act[0]
        back = nn(rin[weights], back.astype(BF16))
        return -2.0 * jnp.sum(back * widths * basis, axis=0, keepdims=True)

    def forward(a):
        far = (a >> 2, (a >> 1) & 1, a & 1)
        srow = jnp.concatenate([srt[a, r : r + 1, :] for r in range(DEG)], axis=1)
        cell = srow >> 4
        near = (cell >> 4, (cell >> 2) & 3, cell & 3)
        cells = [(p + 1) & 1 for p in near]
        atom = ((cells[0] * 2 + cells[1]) * 2 + cells[2]) * 16 + (srow & 15)
        device = jnp.zeros((1, EDGES), jnp.int32)
        for p, f, own in zip(near, far, own_cell):
            device = device * 3 + ((p + 1) >> 1) + tile(f * (1 - 2 * own))
        device = jnp.where(srow >= 0, device, -1)
        onehot = mask(rows_iota((ATOMS, EDGES)) == atom)
        ohot[a] = onehot
        found = nn(places, jnp.concatenate([onehot, onehot], axis=0))
        holds = jnp.where((rows_iota((112, EDGES)) >> 2) == device, 1.0, 0.0)
        nqs[a] = holds.astype(BF16)
        found = holds * found
        total = found[0:8]
        for i in range(1, 14):
            total = total + found[i * 8 : i * 8 + 8]
        total = total[0:4] + total[4:8]
        rel = []
        for k in range(3):
            step = (near[k] - 1 - tile(own_cell[k])).astype(F32)
            rel.append(step + (total[k : k + 1] - tile(sel[a, 4 + k : 5 + k, :])) / CELL)
            rls[a, k : k + 1, :] = rel[k]
        squared = rel[0] * rel[0] + rel[1] * rel[1] + rel[2] * rel[2]
        basis = jnp.exp(-squared * widths)
        bas[a] = basis
        weights = radial(0, basis.astype(BF16), act.at[a])
        kinds = jnp.where(srow >= 0, total[3:4].astype(jnp.int32), -1)
        kept = tn(embp[...].astype(BF16), mask(rows_iota((KINDS, EDGES)) == kinds))
        usrc[a] = kept
        where = slice(a * ATOMS, (a + 1) * ATOMS)
        scl[0:C, where] = (fold(weights[:C] * kept) * RSQRT).astype(BF16)
        vector = weights[C:] * kept
        vec[a] = vector
        for k in range(3):
            scl[(k + 1) * C : (k + 2) * C, where] = (fold(vector * rel[k]) * RSQRT).astype(BF16)

    for a in range(CHUNKS):
        forward(a)

    scalars, mixed_slope = silu(tn(mix1[0], scl[:C]))
    hidden = [scalars.astype(BF16)]
    hidden += [tn(mix1[1], scl[k * C : (k + 1) * C]).astype(BF16) for k in range(1, 4)]
    lifted = [tn(proj[min(k, 1)], hidden[k]).astype(BF16) for k in range(4)]

    rad2[...] = radial(1, bas[0].astype(BF16), act2)
    rel = [rls[0, k : k + 1, :] for k in range(3)]
    for k in range(4):
        lg[k * C : (k + 1) * C, :] = nn(lifted[k], gt[...])
    inner_sum = rel[0] * lg[C : 2 * C] + rel[1] * lg[2 * C : 3 * C] + rel[2] * lg[3 * C :]
    summed_two = fold(rad2[:C] * lg[:C] + rad2[C:] * inner_sum)
    rows = tn(mix2[...], (summed_two * RSQRT).astype(BF16)) + scalars[:, :ATOMS]
    energy, slope = silu(rows)
    local = jnp.sum(energy * weight, axis=0, keepdims=True)
    local = jnp.sum(local, axis=1, keepdims=True)
    grad_rows = weight * slope
    grad = tile(nn(mix2[...], grad_rows.astype(BF16)) * RSQRT)

    def share(axis, buffer, value, first):
        buffer[me[axis]] = jnp.broadcast_to(value, (1, ATOMS))
        copies = []
        for d in range(1, sizes[axis]):
            here = buffer.at[me[axis]]
            copy = remote(
                here, here, en_s.at[first + d - 1], en_r.at[first + d - 1], axis_offset(axis, d)
            )
            copy.start()
            copies.append(copy)
        pending.extend(copies)
        return copies

    def gathered(axis, buffer, copies):
        for copy in copies:
            copy.wait_recv()
        total = buffer[0]
        for i in range(1, sizes[axis]):
            total = total + buffer[i]
        return total[:, 0:1]

    e_copies = share(2, esz, local, sizes[0] + sizes[1])

    grad_inner = grad * rad2[C:]
    dl[:C] = (grad * rad2[:C]).astype(BF16)
    for k in range(3):
        dl[(k + 1) * C : (k + 2) * C] = (grad_inner * rel[k]).astype(BF16)
    back = [nn(dl[k * C : (k + 1) * C], gtt[...]) for k in range(4)]
    pull = radial_back(
        1,
        jnp.concatenate([grad * lg[:C], grad * inner_sum], axis=0).astype(BF16),
        bas[0],
        act2,
    )
    for k in range(3):
        direct = jnp.sum(grad_inner * lg[(k + 1) * C : (k + 2) * C], axis=0, keepdims=True)
        drs[k : k + 1, :] = rel[k] * pull + direct

    back = [nn(proj[min(k, 1)], back[k].astype(BF16)) for k in range(4)]
    own_rows = jnp.concatenate([grad_rows, jnp.zeros((C, 1024 - ATOMS), F32)], axis=1)
    back[0] = (back[0] + own_rows) * mixed_slope
    for k in range(4):
        gsum[k * C : (k + 1) * C] = nn(mix1[min(k, 1)], back[k].astype(BF16)) * RSQRT

    def backward(a):
        where = slice(a * ATOMS, (a + 1) * ATOMS)
        grads = [tile(gsum[k * C : (k + 1) * C, where]) for k in range(4)]
        rel = [rls[a, k : k + 1, :] for k in range(3)]
        towards = rel[0] * grads[1] + rel[1] * grads[2] + rel[2] * grads[3]
        kept = usrc[a]
        pull = radial_back(
            0,
            jnp.concatenate([grads[0] * kept, towards * kept], axis=0).astype(BF16),
            bas[a],
            act.at[a],
        )
        vector = vec[a]
        moved = []
        for k in range(3):
            direct = jnp.sum(vector * grads[k + 1], axis=0, keepdims=True)
            pulled = rel[k] * pull + direct
            if a == 0:
                pulled = pulled + drs[k : k + 1, :]
            moved.append(pulled / CELL)
            tgs[a, k : k + 1, :] = fold(moved[k])
        moved.append(jnp.zeros((1, EDGES), F32))
        moved = jnp.concatenate(moved * 4, axis=0).astype(BF16)
        spread = jnp.concatenate([moved] * 7, axis=0) * nqs[a]
        return nt(spread, ohot[a])

    tgs[...] = jnp.zeros((CHUNKS, 4, ATOMS), F32)
    spreads = []
    for a in range(CHUNKS):
        if a == 6:
            e_copies = share(1, esy, gathered(2, esz, e_copies), sizes[0])
        spreads.append(backward(a))
    pgs[...] = sum(spreads)

    pos_copies = []
    e_copies = share(0, esx, gathered(1, esy, e_copies), 0)
    for d in itertools.product((-1, 0, 1), repeat=3):
        n = place(d)
        pgx[n] = pgs[n * 4 : n * 4 + 4, :] - jnp.where(lanes_of(d), tgs[chunk_of(d)], 0.0)
    for i, d in enumerate(NEIGHBOURS):
        there = place(tuple(-k for k in d))
        copy = remote(pgx.at[place(d)], pr.at[there], pos_s.at[i], pos_r.at[i], d)
        copy.start()
        pos_copies.append(copy)
    pending += pos_copies
    for copy in pos_copies:
        copy.wait_recv()
    total = pgx[mine]
    for d in NEIGHBOURS:
        total = total + pr[place(d)]
    for i, (x, y, z) in enumerate(OWN_CELLS):
        for k in range(3):
            frc[k, x, y, z : z + 1, :] = -total[k : k + 1, i * 16 : i * 16 + 16]
    eng[...] = gathered(0, esx, e_copies) / float(ATOMS * sizes[0] * sizes[1] * sizes[2])
    for copy in pending:
        copy.wait_send()


def body(sizes, *args):
    hbm = pl.BlockSpec(memory_space=pltpu.HBM)
    vmem = pl.BlockSpec(memory_space=pltpu.VMEM)
    held = [pltpu.VMEM(a.shape, a.dtype) for a in args]
    held[2] = pltpu.SMEM(args[2].shape, args[2].dtype)
    energy_sends = sum(sizes)
    dma = pltpu.SemaphoreType.DMA
    scratch = [
        tuple(held),
        dma((len(args),)),
        pltpu.VMEM((27, 8, 128), F32),
        pltpu.VMEM((8, 8, 128), F32),
        pltpu.VMEM((112, 128), F32),
        pltpu.VMEM((8, 8, 128), jnp.int32),
        pltpu.VMEM((96, 128), F32),
        pltpu.VMEM((8, 8, 1024), F32),
        pltpu.VMEM((8, 3, 1024), F32),
        pltpu.VMEM((8, 112, 1024), BF16),
        pltpu.VMEM((8, 128, 1024), BF16),
        pltpu.VMEM((8, 128, 1024), F32),
        pltpu.VMEM((256, 1024), F32),
        pltpu.VMEM((8, 2, 64, 1024), F32),
        pltpu.VMEM((2, 64, 1024), F32),
        pltpu.VMEM((8, 128, 1024), F32),
        pltpu.VMEM((512, 1024), BF16),
        pltpu.VMEM((1024, 1024), BF16),
        pltpu.VMEM((1024, 1024), BF16),
        pltpu.VMEM((512, 1024), F32),
        pltpu.VMEM((512, 1024), BF16),
        pltpu.VMEM((512, 1024), F32),
        pltpu.VMEM((8, 1024), F32),
        pltpu.VMEM((8, 4, 128), F32),
        pltpu.VMEM((112, 128), F32),
        pltpu.VMEM((27, 4, 128), F32),
        pltpu.VMEM((27, 4, 128), F32),
        pltpu.VMEM((sizes[0], 1, 128), F32),
        pltpu.VMEM((sizes[1], 1, 128), F32),
        pltpu.VMEM((sizes[2], 1, 128), F32),
        dma((26,)),
        dma((26,)),
        dma((26,)),
        dma((26,)),
        dma((energy_sends,)),
        dma((energy_sends,)),
    ]
    forces, energy = pl.pallas_call(
        functools.partial(kernel, sizes),
        out_shape=(
            jax.ShapeDtypeStruct(args[0].shape, F32),
            jax.ShapeDtypeStruct((1, 1), F32),
        ),
        in_specs=[hbm] * len(args),
        out_specs=(vmem, vmem),
        scratch_shapes=scratch,
        compiler_params=pltpu.CompilerParams(
            collective_id=0, has_side_effects=True, vmem_limit_bytes=62 * 1024 * 1024
        ),
    )(*args)
    return forces, energy.reshape(())


def solution(mesh):
    sizes = tuple(mesh.shape[a] for a in AXES)
    in_specs = (
        P(None, "gx", "gy", "gz", None),
        P("gx", "gy", "gz", None),
        P("gx", "gy", "gz"),
        P(None, "gx", "gy", "gz", None),
    ) + (P(),) * 8
    out_specs = (P(None, "gx", "gy", "gz", None), P())
    return jax.shard_map(
        functools.partial(body, sizes),
        mesh=mesh,
        in_specs=in_specs,
        out_specs=out_specs,
        check_vma=False,
    )
```

```python
import functools
import itertools

import jax
import jax.numpy as jnp
from jax import lax
from jax.experimental import pallas as pl
from jax.experimental.pallas import tpu as pltpu
from jax.sharding import PartitionSpec as P

F32 = jnp.float32
BF16 = jnp.bfloat16
MESH = pl.DeviceIdType.MESH
AXES = ("gx", "gy", "gz")

C = 128
CELL = 6.0
DEG = 8
ATOMS = 128
EDGES = 1024
WIDTHS = tuple(0.1 * 30.0 ** (k / 7) for k in range(8))
RSQRT = 1.0 / DEG**0.5

NEIGHBOURS = tuple(
    sorted(
        (d for d in itertools.product((-1, 0, 1), repeat=3) if d != (0, 0, 0)),
        key=lambda d: (-abs(d[2]), -abs(d[0]) - abs(d[1])),
    )
)
OWN_CELLS = tuple(itertools.product(range(2), repeat=3))
CHUNKS = 8
KINDS = 96


def place(d):
    return ((d[0] + 1) * 3 + d[1] + 1) * 3 + d[2] + 1


def chunk_of(d):
    return abs(d[0]) * 4 + abs(d[1]) * 2 + abs(d[2])


def dot(a, b, ca, cb):
    return lax.dot_general(a, b, (((ca,), (cb,)), ((), ())), preferred_element_type=F32)


def nn(a, b):
    return dot(a, b, 1, 0)


def tn(a, b):
    return dot(a, b, 0, 0)


def nt(a, b):
    return dot(a, b, 1, 1)


def rows_iota(shape):
    return lax.broadcasted_iota(jnp.int32, shape, 0)


def lanes_iota(shape):
    return lax.broadcasted_iota(jnp.int32, shape, 1)


def mask(condition):
    return jnp.where(condition, 1.0, 0.0).astype(BF16)


def hot(rows, wanted):
    return jnp.where(tile(rows) == wanted.astype(F32).astype(BF16), BF16(1), BF16(0))


def fold(x):
    total = x[:, :ATOMS]
    for r in range(1, DEG):
        total = total + x[:, r * ATOMS : (r + 1) * ATOMS]
    return total


def tile(x):
    return jnp.concatenate([x] * DEG, axis=1)


def silu_of_half(half):
    up = 1.0 + jnp.tanh(half)
    value = half * up
    gate = 0.5 * up
    return value, gate + value * (1.0 - gate)


def silu(x):
    return silu_of_half(0.5 * x)


def two(x):
    high = x.astype(BF16)
    return high, (x - high.astype(F32)).astype(BF16)


def kernel(
    sizes,
    off,
    spe,
    cnt,
    edg,
    emb,
    rin,
    rhid,
    rout,
    mix1,
    proj,
    mix2,
    rdo,
    frc,
    eng,
    vm,
    in_sem,
    blk,
    sel,
    geo,
    srt,
    embp,
    bas,
    rls,
    nqs,
    ohot,
    vec,
    rad2,
    act,
    act2,
    usrc,
    scl,
    gt,
    gtt,
    lg,
    dl,
    gsum,
    drs,
    numbered,
    by_four,
    tgs,
    pgs,
    pgx,
    pr,
    esx,
    esy,
    esz,
    geo_s,
    geo_r,
    pos_s,
    pos_r,
    en_s,
    en_r,
):
    me = tuple(lax.axis_index(a) for a in AXES)
    incoming = (off, spe, cnt, edg, emb, rin, rhid, rout, mix1, proj, mix2, rdo)
    loads = []
    for i, (src, dst) in enumerate(zip(incoming, vm)):
        loads.append(pltpu.make_async_copy(src, dst, in_sem.at[i]))
    for i in (3, 0, 1, 2, 4, 5, 6, 7, 8, 9, 10, 11):
        loads[i].start()
    off, spe, cnt, edg, emb, rin, rhid, rout, mix1, proj, mix2, rdo = vm

    def at(offset):
        return tuple(lax.rem(m + d + n, n) for m, d, n in zip(me, offset, sizes))

    def remote(src, dst, send, recv, offset):
        return pltpu.make_async_remote_copy(
            src_ref=src,
            dst_ref=dst,
            send_sem=send,
            recv_sem=recv,
            device_id=at(offset),
            device_id_type=MESH,
        )

    def axis_offset(axis, d):
        return tuple(d if k == axis else 0 for k in range(3))

    greeted = list(NEIGHBOURS)
    for axis, n in enumerate(sizes):
        greeted += [axis_offset(axis, d) for d in range(2, n - 1)]
    barrier = pltpu.get_barrier_semaphore()
    for d in greeted:
        pl.semaphore_signal(barrier, inc=1, device_id=at(d), device_id_type=MESH)

    loads[3].wait()
    target = edg[0, 0, 0]
    source = edg[1, 0, 0]
    chosen = mask(rows_iota((ATOMS, EDGES)) == target)
    lane2 = lanes_iota((ATOMS, 2 * ATOMS))
    before = mask((rows_iota((ATOMS, 2 * ATOMS)) < lane2) | (lane2 >= ATOMS))
    high_part = (source >> 3).astype(F32)
    low_part = (source & 7).astype(F32)
    base = jnp.zeros((ATOMS, ATOMS), F32)
    table = jnp.zeros((24, ATOMS), F32)
    for b in range(DEG):
        cut = slice(b * ATOMS, (b + 1) * ATOMS)
        part = chosen[:, cut]
        counted = nn(part, before)
        rank = jnp.sum((counted[:, :ATOMS] + base) * part.astype(F32), axis=0, keepdims=True)
        base = base + counted[:, ATOMS:]
        placed = jnp.where(rows_iota((DEG, ATOMS)).astype(F32) == rank, 1.0, 0.0)
        stacked = jnp.concatenate(
            [placed * high_part[:, cut], placed * low_part[:, cut], placed], axis=0
        ).astype(BF16)
        table = table + nt(stacked, part)
    found = table[0:8] * 8.0 + table[8:16] + table[16:24]
    mine = place((0, 0, 0))
    blk[mine, 0:4, :] = found[0:4] * 2048.0 + found[4:8]

    loads[0].wait()
    loads[1].wait()
    for i, (x, y, z) in enumerate(OWN_CELLS):
        here = slice(i * 16, i * 16 + 16)
        for k in range(3):
            blk[mine, 4 + k : 5 + k, here] = off[k, x, y, z : z + 1, :]
        blk[mine, 7:8, here] = spe[x, y, z : z + 1, :].astype(F32)

    pl.semaphore_wait(barrier, len(greeted))
    pending = []
    geo_copies = []
    for i, d in enumerate(NEIGHBOURS):
        there = place(tuple(-k for k in d))
        copy = remote(blk.at[mine], blk.at[there], geo_s.at[i], geo_r.at[i], d)
        copy.start()
        geo_copies.append(copy)
    pending += geo_copies

    for i in (2, 4, 5, 6, 7, 8, 9, 10, 11):
        loads[i].wait()
    half_in = [(0.5 * rin[k].astype(F32)).astype(BF16) for k in range(2)]
    half_hid = [(0.5 * rhid[k].astype(F32)).astype(BF16) for k in range(2)]
    embp[...] = jnp.zeros((KINDS, C), F32)
    embp[0:89, :] = emb[...].astype(F32)
    geo[...] = jnp.zeros((112, ATOMS), F32)
    adds = mask((lanes_iota((8, 3 * C)) >> 7) == rows_iota((8, 3 * C)))
    numbered[...] = rows_iota((ATOMS, ATOMS)).astype(F32).astype(BF16)
    by_four[...] = (rows_iota((112, ATOMS)) >> 2).astype(F32).astype(BF16)
    widths = jnp.zeros((8, EDGES), F32)
    for k in range(8):
        widths = jnp.where(rows_iota((8, EDGES)) == k, WIDTHS[k], widths)
    own_lane = lanes_iota((1, ATOMS))
    own_cell = (own_lane >> 6, (own_lane >> 5) & 1, (own_lane >> 4) & 1)
    readout = jnp.broadcast_to(rdo[...].reshape(1, C), (C, C)).T
    occupied = jnp.zeros((1, ATOMS), F32)
    for i, (x, y, z) in enumerate(OWN_CELLS):
        here = ((own_lane >> 4) == i) & ((own_lane & 15) < cnt[x, y, z])
        occupied = jnp.where(here, 1.0, occupied)
    weight = readout * occupied

    source_row = found.astype(jnp.int32) - 1
    srt[0] = source_row
    cell = source_row >> 4
    near = (cell >> 4, (cell >> 2) & 3, cell & 3)
    chunk = jnp.zeros((DEG, ATOMS), jnp.int32)
    atom = jnp.zeros((DEG, ATOMS), jnp.int32)
    for p in near:
        chunk = chunk * 2 + 1 - (((p + 1) >> 1) & 1)
        atom = atom * 2 + ((p + 1) & 1)
    row = jnp.where(source_row >= 0, chunk * ATOMS + atom * 16 + (source_row & 15), -1)
    srt[1] = row
    column = row.astype(F32).T
    for r in range(DEG):
        cut = slice(r * ATOMS, (r + 1) * ATOMS)
        gt[:, cut] = mask(rows_iota((1024, ATOMS)) == srt[1, r : r + 1, :])
        at_lane = lanes_iota((ATOMS, 1024)).astype(F32)
        gtt[cut, :] = mask(at_lane == column[:, r : r + 1])

    def lanes_of(d):
        chosen = own_lane >= 0
        for step, cell in zip(d, own_cell):
            if step:
                chosen = chosen & (cell == (0 if step > 0 else 1))
        return chosen

    for copy in geo_copies:
        copy.wait_recv()
    gathered_blocks = [jnp.zeros((8, ATOMS), F32)] * CHUNKS
    for d in itertools.product((-1, 0, 1), repeat=3):
        n = place(d)
        block = blk[n]
        geo[n * 4 : n * 4 + 4, :] = block[4:8]
        a = chunk_of(d)
        gathered_blocks[a] = jnp.where(lanes_of(d), block, gathered_blocks[a])
    for a in range(CHUNKS):
        sel[a] = gathered_blocks[a]
        if a:
            packed = gathered_blocks[a][0:4].astype(jnp.int32)
            srt[a] = jnp.concatenate([packed >> 11, packed & 2047], axis=0) - 1
    places = jnp.concatenate(two(geo[...]), axis=1)

    def radial(weights, basis_low, act):
        first, slope = silu_of_half(tn(half_in[weights], basis_low))
        act[0] = slope
        second, slope = silu_of_half(tn(half_hid[weights], first.astype(BF16)))
        act[1] = slope
        return tn(rout[weights], second.astype(BF16))

    def radial_back(weights, grad, basis, act):
        back = nn(rout[weights], grad) * act[1]
        back = nn(rhid[weights], back.astype(BF16)) * act[0]
        back = nn(rin[weights], back.astype(BF16))
        return -2.0 * jnp.sum(back * widths * basis, axis=0, keepdims=True)

    def forward(a):
        far = (a >> 2, (a >> 1) & 1, a & 1)
        srow = jnp.concatenate([srt[a, r : r + 1, :] for r in range(DEG)], axis=1)
        cell = srow >> 4
        near = (cell >> 4, (cell >> 2) & 3, cell & 3)
        cells = [(p + 1) & 1 for p in near]
        atom = ((cells[0] * 2 + cells[1]) * 2 + cells[2]) * 16 + (srow & 15)
        device = jnp.zeros((1, EDGES), jnp.int32)
        for p, f, own in zip(near, far, own_cell):
            device = device * 3 + ((p + 1) >> 1) + tile(f * (1 - 2 * own))
        device = jnp.where(srow >= 0, device, -1)
        onehot = hot(numbered[...], atom)
        ohot[a] = onehot
        found = nn(places, jnp.concatenate([onehot, onehot], axis=0))
        nqs[a] = hot(by_four[...], device)
        found = jnp.where((rows_iota((112, EDGES)) >> 2) == device, found, 0.0)
        total = found[0:8]
        for i in range(1, 14):
            total = total + found[i * 8 : i * 8 + 8]
        total = total[0:4] + total[4:8]
        rel = []
        for k in range(3):
            step = (near[k] - 1 - tile(own_cell[k])).astype(F32)
            rel.append(step + (total[k : k + 1] - tile(sel[a, 4 + k : 5 + k, :])) / CELL)
            rls[a, k : k + 1, :] = rel[k]
        squared = rel[0] * rel[0] + rel[1] * rel[1] + rel[2] * rel[2]
        basis = jnp.exp(-squared * widths)
        bas[a] = basis
        weights = radial(0, basis.astype(BF16), act.at[a])
        kinds = jnp.where(srow >= 0, total[3:4].astype(jnp.int32), -1)
        kept = tn(embp[...].astype(BF16), hot(numbered[0:KINDS, :], kinds))
        usrc[a] = kept.astype(BF16)
        where = slice(a * ATOMS, (a + 1) * ATOMS)
        scl[0:C, where] = (fold(weights[:C] * kept) * RSQRT).astype(BF16)
        vector = weights[C:] * kept
        vec[a] = vector.astype(BF16)
        for k in range(3):
            scl[(k + 1) * C : (k + 2) * C, where] = (fold(vector * rel[k]) * RSQRT).astype(BF16)

    for a in range(CHUNKS):
        forward(a)

    scalars, mixed_slope = silu(tn(mix1[0], scl[:C]))
    hidden = [scalars.astype(BF16)]
    hidden += [tn(mix1[1], scl[k * C : (k + 1) * C]).astype(BF16) for k in range(1, 4)]
    lifted = [tn(proj[min(k, 1)], hidden[k]).astype(BF16) for k in range(4)]

    rad2[...] = radial(1, bas[0].astype(BF16), act2)
    rel = [rls[0, k : k + 1, :] for k in range(3)]
    lg[...] = nn(jnp.concatenate(lifted, axis=0), gt[...])
    inner_sum = rel[0] * lg[C : 2 * C] + rel[1] * lg[2 * C : 3 * C] + rel[2] * lg[3 * C :]
    summed_two = fold(rad2[:C] * lg[:C] + rad2[C:] * inner_sum)
    rows = tn(mix2[...], (summed_two * RSQRT).astype(BF16)) + scalars[:, :ATOMS]
    energy, slope = silu(rows)
    local = jnp.sum(energy * weight, axis=0, keepdims=True)
    local = jnp.sum(local, axis=1, keepdims=True)
    grad_rows = weight * slope
    grad = tile(nn(mix2[...], grad_rows.astype(BF16)) * RSQRT)

    def share(axis, buffer, value, first):
        buffer[me[axis]] = jnp.broadcast_to(value, (1, ATOMS))
        copies = []
        for d in range(1, sizes[axis]):
            here = buffer.at[me[axis]]
            copy = remote(
                here, here, en_s.at[first + d - 1], en_r.at[first + d - 1], axis_offset(axis, d)
            )
            copy.start()
            copies.append(copy)
        pending.extend(copies)
        return copies

    def gathered(axis, buffer, copies):
        for copy in copies:
            copy.wait_recv()
        total = buffer[0]
        for i in range(1, sizes[axis]):
            total = total + buffer[i]
        return total[:, 0:1]

    e_copies = share(2, esz, local, sizes[0] + sizes[1])

    grad_inner = grad * rad2[C:]
    dl[:C] = (grad * rad2[:C]).astype(BF16)
    for k in range(3):
        dl[(k + 1) * C : (k + 2) * C] = (grad_inner * rel[k]).astype(BF16)
    back = nn(dl[...], gtt[...]).astype(BF16)
    pull = radial_back(
        1,
        jnp.concatenate([grad * lg[:C], grad * inner_sum], axis=0).astype(BF16),
        bas[0],
        act2,
    )
    for k in range(3):
        direct = jnp.sum(grad_inner * lg[(k + 1) * C : (k + 2) * C], axis=0, keepdims=True)
        drs[k : k + 1, :] = rel[k] * pull + direct

    back = [nn(proj[min(k, 1)], back[k * C : (k + 1) * C]) for k in range(4)]
    own_rows = jnp.concatenate([grad_rows, jnp.zeros((C, 1024 - ATOMS), F32)], axis=1)
    back[0] = (back[0] + own_rows) * mixed_slope
    for k in range(4):
        grown = nn(mix1[min(k, 1)], back[k].astype(BF16)) * RSQRT
        gsum[k * C : (k + 1) * C] = grown.astype(BF16)

    def backward(a):
        where = slice(a * ATOMS, (a + 1) * ATOMS)
        grads = [tile(gsum[k * C : (k + 1) * C, where]) for k in range(4)]
        rel = [rls[a, k : k + 1, :] for k in range(3)]
        low = [r.astype(BF16) for r in rel]
        towards = low[0] * grads[1] + low[1] * grads[2] + low[2] * grads[3]
        kept = usrc[a]
        pull = radial_back(
            0,
            jnp.concatenate([grads[0] * kept, towards * kept], axis=0),
            bas[a],
            act.at[a],
        )
        vector = vec[a]
        direct = nn(adds, jnp.concatenate([vector * g for g in grads[1:]], axis=0))
        moved = []
        for k in range(3):
            pulled = rel[k] * pull + direct[k : k + 1]
            if a == 0:
                pulled = pulled + drs[k : k + 1, :]
            moved.append(pulled / CELL)
            tgs[a, k : k + 1, :] = fold(moved[k])
        moved.append(jnp.zeros((1, EDGES), F32))
        moved = jnp.concatenate(moved * 4, axis=0).astype(BF16)
        spread = jnp.concatenate([moved] * 7, axis=0) * nqs[a]
        return nt(spread, ohot[a])

    tgs[...] = jnp.zeros((CHUNKS, 4, ATOMS), F32)
    spreads = []
    for a in range(CHUNKS):
        spreads.append(backward(a))
    pgs[...] = sum(spreads)

    pos_copies = []
    for d in itertools.product((-1, 0, 1), repeat=3):
        n = place(d)
        pgx[n] = pgs[n * 4 : n * 4 + 4, :] - jnp.where(lanes_of(d), tgs[chunk_of(d)], 0.0)
    for i, d in enumerate(NEIGHBOURS):
        there = place(tuple(-k for k in d))
        copy = remote(pgx.at[place(d)], pr.at[there], pos_s.at[i], pos_r.at[i], d)
        copy.start()
        pos_copies.append(copy)
    pending += pos_copies
    e_copies = share(1, esy, gathered(2, esz, e_copies), sizes[0])
    e_copies = share(0, esx, gathered(1, esy, e_copies), 0)
    for copy in pos_copies:
        copy.wait_recv()
    total = pgx[mine]
    for d in NEIGHBOURS:
        total = total + pr[place(d)]
    for i, (x, y, z) in enumerate(OWN_CELLS):
        for k in range(3):
            frc[k, x, y, z : z + 1, :] = -total[k : k + 1, i * 16 : i * 16 + 16]
    eng[...] = gathered(0, esx, e_copies) / float(ATOMS * sizes[0] * sizes[1] * sizes[2])
    for copy in pending:
        copy.wait_send()


def body(sizes, *args):
    hbm = pl.BlockSpec(memory_space=pltpu.HBM)
    vmem = pl.BlockSpec(memory_space=pltpu.VMEM)
    held = [pltpu.VMEM(a.shape, a.dtype) for a in args]
    held[2] = pltpu.SMEM(args[2].shape, args[2].dtype)
    energy_sends = sum(sizes)
    dma = pltpu.SemaphoreType.DMA
    scratch = [
        tuple(held),
        dma((len(args),)),
        pltpu.VMEM((27, 8, 128), F32),
        pltpu.VMEM((8, 8, 128), F32),
        pltpu.VMEM((112, 128), F32),
        pltpu.VMEM((8, 8, 128), jnp.int32),
        pltpu.VMEM((96, 128), F32),
        pltpu.VMEM((8, 8, 1024), F32),
        pltpu.VMEM((8, 3, 1024), F32),
        pltpu.VMEM((8, 112, 1024), BF16),
        pltpu.VMEM((8, 128, 1024), BF16),
        pltpu.VMEM((8, 128, 1024), BF16),
        pltpu.VMEM((256, 1024), F32),
        pltpu.VMEM((8, 2, 64, 1024), F32),
        pltpu.VMEM((2, 64, 1024), F32),
        pltpu.VMEM((8, 128, 1024), BF16),
        pltpu.VMEM((512, 1024), BF16),
        pltpu.VMEM((1024, 1024), BF16),
        pltpu.VMEM((1024, 1024), BF16),
        pltpu.VMEM((512, 1024), F32),
        pltpu.VMEM((512, 1024), BF16),
        pltpu.VMEM((512, 1024), BF16),
        pltpu.VMEM((8, 1024), F32),
        pltpu.VMEM((128, 128), BF16),
        pltpu.VMEM((112, 128), BF16),
        pltpu.VMEM((8, 4, 128), F32),
        pltpu.VMEM((112, 128), F32),
        pltpu.VMEM((27, 4, 128), F32),
        pltpu.VMEM((27, 4, 128), F32),
        pltpu.VMEM((sizes[0], 1, 128), F32),
        pltpu.VMEM((sizes[1], 1, 128), F32),
        pltpu.VMEM((sizes[2], 1, 128), F32),
        dma((26,)),
        dma((26,)),
        dma((26,)),
        dma((26,)),
        dma((energy_sends,)),
        dma((energy_sends,)),
    ]
    forces, energy = pl.pallas_call(
        functools.partial(kernel, sizes),
        out_shape=(
            jax.ShapeDtypeStruct(args[0].shape, F32),
            jax.ShapeDtypeStruct((1, 1), F32),
        ),
        in_specs=[hbm] * len(args),
        out_specs=(vmem, vmem),
        scratch_shapes=scratch,
        compiler_params=pltpu.CompilerParams(
            collective_id=0, has_side_effects=True, vmem_limit_bytes=62 * 1024 * 1024
        ),
    )(*args)
    return forces, energy.reshape(())


def solution(mesh):
    sizes = tuple(mesh.shape[a] for a in AXES)
    in_specs = (
        P(None, "gx", "gy", "gz", None),
        P("gx", "gy", "gz", None),
        P("gx", "gy", "gz"),
        P(None, "gx", "gy", "gz", None),
    ) + (P(),) * 8
    out_specs = (P(None, "gx", "gy", "gz", None), P())
    return jax.shard_map(
        functools.partial(body, sizes),
        mesh=mesh,
        in_specs=in_specs,
        out_specs=out_specs,
        check_vma=False,
    )
```

```python
import functools
import itertools

import jax
import jax.numpy as jnp
from jax import lax
from jax.experimental import pallas as pl
from jax.experimental.pallas import tpu as pltpu
from jax.sharding import PartitionSpec as P

F32 = jnp.float32
BF16 = jnp.bfloat16
MESH = pl.DeviceIdType.MESH
AXES = ("gx", "gy", "gz")

C = 128
CELL = 6.0
DEG = 8
ATOMS = 128
EDGES = 1024
WIDTHS = tuple(0.1 * 30.0 ** (k / 7) for k in range(8))
RSQRT = 1.0 / DEG**0.5

NEIGHBOURS = tuple(
    sorted(
        (d for d in itertools.product((-1, 0, 1), repeat=3) if d != (0, 0, 0)),
        key=lambda d: (-abs(d[2]), -abs(d[0]) - abs(d[1])),
    )
)
OWN_CELLS = tuple(itertools.product(range(2), repeat=3))
CHUNKS = 8
KINDS = 96


def place(d):
    return ((d[0] + 1) * 3 + d[1] + 1) * 3 + d[2] + 1


def chunk_of(d):
    return abs(d[0]) * 4 + abs(d[1]) * 2 + abs(d[2])


def dot(a, b, ca, cb):
    return lax.dot_general(a, b, (((ca,), (cb,)), ((), ())), preferred_element_type=F32)


def nn(a, b):
    return dot(a, b, 1, 0)


def tn(a, b):
    return dot(a, b, 0, 0)


def nt(a, b):
    return dot(a, b, 1, 1)


def rows_iota(shape):
    return lax.broadcasted_iota(jnp.int32, shape, 0)


def lanes_iota(shape):
    return lax.broadcasted_iota(jnp.int32, shape, 1)


def mask(condition):
    return jnp.where(condition, 1.0, 0.0).astype(BF16)


def hot(rows, wanted):
    return jnp.where(tile(rows) == wanted.astype(F32).astype(BF16), BF16(1), BF16(0))


def fold(x):
    total = x[:, :ATOMS]
    for r in range(1, DEG):
        total = total + x[:, r * ATOMS : (r + 1) * ATOMS]
    return total


def tile(x):
    return jnp.concatenate([x] * DEG, axis=1)


def silu_of_half(half):
    up = 1.0 + jnp.tanh(half)
    value = (half * up).astype(BF16)
    gate = BF16(0.5) * up.astype(BF16)
    return value, gate + value * (BF16(1) - gate)


def silu(x):
    half = 0.5 * x
    up = 1.0 + jnp.tanh(half)
    value = half * up
    gate = 0.5 * up
    return value, gate + value * (1.0 - gate)


def run(steps):
    while True:
        try:
            next(steps)
        except StopIteration as end:
            return end.value


def in_turns(several, depth):
    waiting, active = list(several), []
    while waiting or active:
        if waiting and len(active) < depth:
            active.append(waiting.pop(0))
        for steps in tuple(active):
            if next(steps, True):
                active.remove(steps)


def two(x):
    high = x.astype(BF16)
    return high, (x - high.astype(F32)).astype(BF16)


def kernel(
    sizes,
    off,
    spe,
    cnt,
    edg,
    emb,
    rin,
    rhid,
    rout,
    mix1,
    proj,
    mix2,
    rdo,
    frc,
    eng,
    vm,
    in_sem,
    blk,
    sel,
    geo,
    srt,
    embp,
    bas,
    rls,
    nqs,
    ohot,
    vec,
    rad2,
    act,
    act2,
    usrc,
    scl,
    gt,
    gtt,
    lg,
    dl,
    gsum,
    drs,
    numbered,
    by_four,
    tgs,
    pgs,
    pgx,
    pr,
    esx,
    esy,
    esz,
    geo_s,
    geo_r,
    pos_s,
    pos_r,
    en_s,
    en_r,
):
    me = tuple(lax.axis_index(a) for a in AXES)
    incoming = (off, spe, cnt, edg, emb, rin, rhid, rout, mix1, proj, mix2, rdo)
    loads = []
    for i, (src, dst) in enumerate(zip(incoming, vm)):
        loads.append(pltpu.make_async_copy(src, dst, in_sem.at[i]))
    for i in (3, 0, 1, 2, 4, 5, 6, 7, 8, 9, 10, 11):
        loads[i].start()
    off, spe, cnt, edg, emb, rin, rhid, rout, mix1, proj, mix2, rdo = vm

    def at(offset):
        return tuple(lax.rem(m + d + n, n) for m, d, n in zip(me, offset, sizes))

    def remote(src, dst, send, recv, offset):
        return pltpu.make_async_remote_copy(
            src_ref=src,
            dst_ref=dst,
            send_sem=send,
            recv_sem=recv,
            device_id=at(offset),
            device_id_type=MESH,
        )

    def axis_offset(axis, d):
        return tuple(d if k == axis else 0 for k in range(3))

    greeted = list(NEIGHBOURS)
    for axis, n in enumerate(sizes):
        greeted += [axis_offset(axis, d) for d in range(2, n - 1)]
    barrier = pltpu.get_barrier_semaphore()
    for d in greeted:
        pl.semaphore_signal(barrier, inc=1, device_id=at(d), device_id_type=MESH)

    loads[3].wait()
    target = edg[0, 0, 0]
    source = edg[1, 0, 0]
    chosen = mask(rows_iota((ATOMS, EDGES)) == target)
    lane2 = lanes_iota((ATOMS, 2 * ATOMS))
    before = mask((rows_iota((ATOMS, 2 * ATOMS)) < lane2) | (lane2 >= ATOMS))
    high_part = (source >> 3).astype(F32)
    low_part = (source & 7).astype(F32)
    base = jnp.zeros((ATOMS, ATOMS), F32)
    table = jnp.zeros((24, ATOMS), F32)
    for b in range(DEG):
        cut = slice(b * ATOMS, (b + 1) * ATOMS)
        part = chosen[:, cut]
        counted = nn(part, before)
        rank = jnp.sum((counted[:, :ATOMS] + base) * part.astype(F32), axis=0, keepdims=True)
        base = base + counted[:, ATOMS:]
        placed = jnp.where(rows_iota((DEG, ATOMS)).astype(F32) == rank, 1.0, 0.0)
        stacked = jnp.concatenate(
            [placed * high_part[:, cut], placed * low_part[:, cut], placed], axis=0
        ).astype(BF16)
        table = table + nt(stacked, part)
    found = table[0:8] * 8.0 + table[8:16] + table[16:24]
    mine = place((0, 0, 0))
    blk[mine, 0:4, :] = found[0:4] * 2048.0 + found[4:8]

    loads[0].wait()
    loads[1].wait()
    for i, (x, y, z) in enumerate(OWN_CELLS):
        here = slice(i * 16, i * 16 + 16)
        for k in range(3):
            blk[mine, 4 + k : 5 + k, here] = off[k, x, y, z : z + 1, :]
        blk[mine, 7:8, here] = spe[x, y, z : z + 1, :].astype(F32)

    pl.semaphore_wait(barrier, len(greeted))
    pending = []
    geo_copies = []
    for i, d in enumerate(NEIGHBOURS):
        there = place(tuple(-k for k in d))
        copy = remote(blk.at[mine], blk.at[there], geo_s.at[i], geo_r.at[i], d)
        copy.start()
        geo_copies.append(copy)
    pending += geo_copies

    for i in (2, 4, 5, 6, 7, 8, 9, 10, 11):
        loads[i].wait()
    half_in = [(0.5 * rin[k].astype(F32)).astype(BF16) for k in range(2)]
    half_hid = [(0.5 * rhid[k].astype(F32)).astype(BF16) for k in range(2)]
    joined = nn(mix1[1], proj[1]).astype(BF16)
    embp[...] = jnp.zeros((KINDS, C), F32)
    embp[0:89, :] = emb[...].astype(F32)
    geo[...] = jnp.zeros((112, ATOMS), F32)
    adds = mask((lanes_iota((8, 3 * C)) >> 7) == rows_iota((8, 3 * C)))
    numbered[...] = rows_iota((ATOMS, ATOMS)).astype(F32).astype(BF16)
    by_four[...] = (rows_iota((112, ATOMS)) >> 2).astype(F32).astype(BF16)
    widths = jnp.zeros((8, EDGES), F32)
    for k in range(8):
        widths = jnp.where(rows_iota((8, EDGES)) == k, WIDTHS[k], widths)
    own_lane = lanes_iota((1, ATOMS))
    own_cell = (own_lane >> 6, (own_lane >> 5) & 1, (own_lane >> 4) & 1)
    readout = jnp.broadcast_to(rdo[...].reshape(1, C), (C, C)).T
    occupied = jnp.zeros((1, ATOMS), F32)
    for i, (x, y, z) in enumerate(OWN_CELLS):
        here = ((own_lane >> 4) == i) & ((own_lane & 15) < cnt[x, y, z])
        occupied = jnp.where(here, 1.0, occupied)
    weight = readout * occupied

    source_row = found.astype(jnp.int32) - 1
    srt[0] = source_row
    cell = source_row >> 4
    near = (cell >> 4, (cell >> 2) & 3, cell & 3)
    chunk = jnp.zeros((DEG, ATOMS), jnp.int32)
    atom = jnp.zeros((DEG, ATOMS), jnp.int32)
    for p in near:
        chunk = chunk * 2 + 1 - (((p + 1) >> 1) & 1)
        atom = atom * 2 + ((p + 1) & 1)
    row = jnp.where(source_row >= 0, chunk * ATOMS + atom * 16 + (source_row & 15), -1)
    srt[1] = row
    column = row.astype(F32).T
    for r in range(DEG):
        cut = slice(r * ATOMS, (r + 1) * ATOMS)
        gt[:, cut] = mask(rows_iota((1024, ATOMS)) == srt[1, r : r + 1, :])
        at_lane = lanes_iota((ATOMS, 1024)).astype(F32)
        gtt[cut, :] = mask(at_lane == column[:, r : r + 1])

    def lanes_of(d):
        chosen = own_lane >= 0
        for step, cell in zip(d, own_cell):
            if step:
                chosen = chosen & (cell == (0 if step > 0 else 1))
        return chosen

    for copy in geo_copies:
        copy.wait_recv()
    gathered_blocks = [jnp.zeros((8, ATOMS), F32)] * CHUNKS
    for d in itertools.product((-1, 0, 1), repeat=3):
        n = place(d)
        block = blk[n]
        geo[n * 4 : n * 4 + 4, :] = block[4:8]
        a = chunk_of(d)
        gathered_blocks[a] = jnp.where(lanes_of(d), block, gathered_blocks[a])
    for a in range(CHUNKS):
        sel[a] = gathered_blocks[a]
        if a:
            packed = gathered_blocks[a][0:4].astype(jnp.int32)
            srt[a] = jnp.concatenate([packed >> 11, packed & 2047], axis=0) - 1
    places = jnp.concatenate(two(geo[...]), axis=1)

    def radial(weights, basis_low, act):
        first = tn(half_in[weights], basis_low)
        yield
        first, slope = silu_of_half(first)
        act[0] = slope
        second = tn(half_hid[weights], first)
        yield
        second, slope = silu_of_half(second)
        act[1] = slope
        out = tn(rout[weights], second)
        yield
        return out

    def radial_back(weights, grad, basis, act):
        back = nn(rout[weights], grad)
        yield
        back = nn(rhid[weights], back.astype(BF16) * act[1])
        yield
        back = nn(rin[weights], back.astype(BF16) * act[0])
        yield
        return -2.0 * jnp.sum(back * widths * basis, axis=0, keepdims=True)

    def forward(a):
        far = (a >> 2, (a >> 1) & 1, a & 1)
        srow = jnp.concatenate([srt[a, r : r + 1, :] for r in range(DEG)], axis=1)
        cell = srow >> 4
        near = (cell >> 4, (cell >> 2) & 3, cell & 3)
        cells = [(p + 1) & 1 for p in near]
        atom = ((cells[0] * 2 + cells[1]) * 2 + cells[2]) * 16 + (srow & 15)
        device = jnp.zeros((1, EDGES), jnp.int32)
        for p, f, own in zip(near, far, own_cell):
            device = device * 3 + ((p + 1) >> 1) + tile(f * (1 - 2 * own))
        device = jnp.where(srow >= 0, device, -1)
        onehot = hot(numbered[...], atom)
        ohot[a] = onehot
        found = nn(places, jnp.concatenate([onehot, onehot], axis=0))
        yield
        nqs[a] = hot(by_four[...], device)
        found = jnp.where((rows_iota((112, EDGES)) >> 2) == device, found, 0.0)
        total = found[0:8]
        for i in range(1, 14):
            total = total + found[i * 8 : i * 8 + 8]
        total = total[0:4] + total[4:8]
        rel = []
        for k in range(3):
            step = (near[k] - 1 - tile(own_cell[k])).astype(F32)
            rel.append(step + (total[k : k + 1] - tile(sel[a, 4 + k : 5 + k, :])) / CELL)
            rls[a, k : k + 1, :] = rel[k]
        squared = rel[0] * rel[0] + rel[1] * rel[1] + rel[2] * rel[2]
        basis = jnp.exp(-squared * widths)
        bas[a] = basis
        weights = yield from radial(0, basis.astype(BF16), act.at[a])
        kinds = jnp.where(srow >= 0, total[3:4].astype(jnp.int32), -1)
        kept = tn(embp[...].astype(BF16), hot(numbered[0:KINDS, :], kinds))
        usrc[a] = kept.astype(BF16)
        where = slice(a * ATOMS, (a + 1) * ATOMS)
        scl[0:C, where] = (fold(weights[:C] * kept) * RSQRT).astype(BF16)
        vector = weights[C:] * kept
        vec[a] = vector.astype(BF16)
        for k in range(3):
            scl[(k + 1) * C : (k + 2) * C, where] = (fold(vector * rel[k]) * RSQRT).astype(BF16)

    in_turns([forward(a) for a in range(CHUNKS)], 3)

    scalars, mixed_slope = silu(tn(mix1[0], scl[:C]))
    lifted = [tn(proj[0], scalars.astype(BF16)).astype(BF16)]
    lifted += [tn(joined, scl[k * C : (k + 1) * C]).astype(BF16) for k in range(1, 4)]

    rad2[...] = run(radial(1, bas[0].astype(BF16), act2))
    rel = [rls[0, k : k + 1, :] for k in range(3)]
    lg[...] = nn(jnp.concatenate(lifted, axis=0), gt[...])
    inner_sum = rel[0] * lg[C : 2 * C] + rel[1] * lg[2 * C : 3 * C] + rel[2] * lg[3 * C :]
    summed_two = fold(rad2[:C] * lg[:C] + rad2[C:] * inner_sum)
    rows = tn(mix2[...], (summed_two * RSQRT).astype(BF16)) + scalars[:, :ATOMS]
    energy, slope = silu(rows)
    local = jnp.sum(energy * weight, axis=0, keepdims=True)
    local = jnp.sum(local, axis=1, keepdims=True)
    grad_rows = weight * slope
    grad = tile(nn(mix2[...], grad_rows.astype(BF16)) * RSQRT)

    def share(axis, buffer, value, first):
        buffer[me[axis]] = jnp.broadcast_to(value, (1, ATOMS))
        copies = []
        for d in range(1, sizes[axis]):
            here = buffer.at[me[axis]]
            copy = remote(
                here, here, en_s.at[first + d - 1], en_r.at[first + d - 1], axis_offset(axis, d)
            )
            copy.start()
            copies.append(copy)
        pending.extend(copies)
        return copies

    def gathered(axis, buffer, copies):
        for copy in copies:
            copy.wait_recv()
        total = buffer[0]
        for i in range(1, sizes[axis]):
            total = total + buffer[i]
        return total[:, 0:1]

    e_copies = share(2, esz, local, sizes[0] + sizes[1])

    grad_inner = grad * rad2[C:]
    dl[:C] = (grad * rad2[:C]).astype(BF16)
    for k in range(3):
        dl[(k + 1) * C : (k + 2) * C] = (grad_inner * rel[k]).astype(BF16)
    back = nn(dl[...], gtt[...]).astype(BF16)
    pull = run(
    radial_back(
        1,
        jnp.concatenate([grad * lg[:C], grad * inner_sum], axis=0).astype(BF16),
        bas[0],
        act2,
    )
    )
    for k in range(3):
        direct = jnp.sum(grad_inner * lg[(k + 1) * C : (k + 2) * C], axis=0, keepdims=True)
        drs[k : k + 1, :] = rel[k] * pull + direct

    own_rows = jnp.concatenate([grad_rows, jnp.zeros((C, 1024 - ATOMS), F32)], axis=1)
    grad_mixed = (nn(proj[0], back[:C]) + own_rows) * mixed_slope
    gsum[:C] = (nn(mix1[0], grad_mixed.astype(BF16)) * RSQRT).astype(BF16)
    for k in range(1, 4):
        cut = slice(k * C, (k + 1) * C)
        gsum[cut] = (nn(joined, back[cut]) * RSQRT).astype(BF16)

    def backward(a):
        where = slice(a * ATOMS, (a + 1) * ATOMS)
        grads = [tile(gsum[k * C : (k + 1) * C, where]) for k in range(4)]
        rel = [rls[a, k : k + 1, :] for k in range(3)]
        low = [r.astype(BF16) for r in rel]
        towards = low[0] * grads[1] + low[1] * grads[2] + low[2] * grads[3]
        kept = usrc[a]
        pull = yield from radial_back(
            0,
            jnp.concatenate([grads[0] * kept, towards * kept], axis=0),
            bas[a],
            act.at[a],
        )
        vector = vec[a]
        direct = nn(adds, jnp.concatenate([vector * g for g in grads[1:]], axis=0))
        moved = []
        for k in range(3):
            pulled = rel[k] * pull + direct[k : k + 1]
            if a == 0:
                pulled = pulled + drs[k : k + 1, :]
            moved.append(pulled / CELL)
            tgs[a, k : k + 1, :] = fold(moved[k])
        moved.append(jnp.zeros((1, EDGES), F32))
        moved = jnp.concatenate(moved * 4, axis=0).astype(BF16)
        spread = jnp.concatenate([moved] * 7, axis=0) * nqs[a]
        spreads.append(nt(spread, ohot[a]))

    tgs[...] = jnp.zeros((CHUNKS, 4, ATOMS), F32)
    spreads = []
    in_turns([backward(a) for a in range(CHUNKS)], 3)
    pgs[...] = sum(spreads)

    pos_copies = []
    for d in itertools.product((-1, 0, 1), repeat=3):
        n = place(d)
        pgx[n] = pgs[n * 4 : n * 4 + 4, :] - jnp.where(lanes_of(d), tgs[chunk_of(d)], 0.0)
    for i, d in enumerate(NEIGHBOURS):
        there = place(tuple(-k for k in d))
        copy = remote(pgx.at[place(d)], pr.at[there], pos_s.at[i], pos_r.at[i], d)
        copy.start()
        pos_copies.append(copy)
    pending += pos_copies
    e_copies = share(1, esy, gathered(2, esz, e_copies), sizes[0])
    e_copies = share(0, esx, gathered(1, esy, e_copies), 0)
    for copy in pos_copies:
        copy.wait_recv()
    total = pgx[mine]
    for d in NEIGHBOURS:
        total = total + pr[place(d)]
    for i, (x, y, z) in enumerate(OWN_CELLS):
        for k in range(3):
            frc[k, x, y, z : z + 1, :] = -total[k : k + 1, i * 16 : i * 16 + 16]
    eng[...] = gathered(0, esx, e_copies) / float(ATOMS * sizes[0] * sizes[1] * sizes[2])
    for copy in pending:
        copy.wait_send()


def body(sizes, *args):
    hbm = pl.BlockSpec(memory_space=pltpu.HBM)
    vmem = pl.BlockSpec(memory_space=pltpu.VMEM)
    held = [pltpu.VMEM(a.shape, a.dtype) for a in args]
    held[2] = pltpu.SMEM(args[2].shape, args[2].dtype)
    energy_sends = sum(sizes)
    dma = pltpu.SemaphoreType.DMA
    scratch = [
        tuple(held),
        dma((len(args),)),
        pltpu.VMEM((27, 8, 128), F32),
        pltpu.VMEM((8, 8, 128), F32),
        pltpu.VMEM((112, 128), F32),
        pltpu.VMEM((8, 8, 128), jnp.int32),
        pltpu.VMEM((96, 128), F32),
        pltpu.VMEM((8, 8, 1024), F32),
        pltpu.VMEM((8, 3, 1024), F32),
        pltpu.VMEM((8, 112, 1024), BF16),
        pltpu.VMEM((8, 128, 1024), BF16),
        pltpu.VMEM((8, 128, 1024), BF16),
        pltpu.VMEM((256, 1024), F32),
        pltpu.VMEM((8, 2, 64, 1024), BF16),
        pltpu.VMEM((2, 64, 1024), BF16),
        pltpu.VMEM((8, 128, 1024), BF16),
        pltpu.VMEM((512, 1024), BF16),
        pltpu.VMEM((1024, 1024), BF16),
        pltpu.VMEM((1024, 1024), BF16),
        pltpu.VMEM((512, 1024), F32),
        pltpu.VMEM((512, 1024), BF16),
        pltpu.VMEM((512, 1024), BF16),
        pltpu.VMEM((8, 1024), F32),
        pltpu.VMEM((128, 128), BF16),
        pltpu.VMEM((112, 128), BF16),
        pltpu.VMEM((8, 4, 128), F32),
        pltpu.VMEM((112, 128), F32),
        pltpu.VMEM((27, 4, 128), F32),
        pltpu.VMEM((27, 4, 128), F32),
        pltpu.VMEM((sizes[0], 1, 128), F32),
        pltpu.VMEM((sizes[1], 1, 128), F32),
        pltpu.VMEM((sizes[2], 1, 128), F32),
        dma((26,)),
        dma((26,)),
        dma((26,)),
        dma((26,)),
        dma((energy_sends,)),
        dma((energy_sends,)),
    ]
    forces, energy = pl.pallas_call(
        functools.partial(kernel, sizes),
        out_shape=(
            jax.ShapeDtypeStruct(args[0].shape, F32),
            jax.ShapeDtypeStruct((1, 1), F32),
        ),
        in_specs=[hbm] * len(args),
        out_specs=(vmem, vmem),
        scratch_shapes=scratch,
        compiler_params=pltpu.CompilerParams(
            collective_id=0, has_side_effects=True, vmem_limit_bytes=62 * 1024 * 1024
        ),
    )(*args)
    return forces, energy.reshape(())


def solution(mesh):
    sizes = tuple(mesh.shape[a] for a in AXES)
    in_specs = (
        P(None, "gx", "gy", "gz", None),
        P("gx", "gy", "gz", None),
        P("gx", "gy", "gz"),
        P(None, "gx", "gy", "gz", None),
    ) + (P(),) * 8
    out_specs = (P(None, "gx", "gy", "gz", None), P())
    return jax.shard_map(
        functools.partial(body, sizes),
        mesh=mesh,
        in_specs=in_specs,
        out_specs=out_specs,
        check_vma=False,
    )
```

```python
import functools
import itertools

import jax
import jax.numpy as jnp
from jax import lax
from jax.experimental import pallas as pl
from jax.experimental.pallas import tpu as pltpu
from jax.sharding import PartitionSpec as P

F32 = jnp.float32
BF16 = jnp.bfloat16
MESH = pl.DeviceIdType.MESH
AXES = ("gx", "gy", "gz")

C = 128
CELL = 6.0
DEG = 8
ATOMS = 128
EDGES = 1024
WIDTHS = tuple(0.1 * 30.0 ** (k / 7) for k in range(8))
RSQRT = 1.0 / DEG**0.5

NEIGHBOURS = tuple(
    sorted(
        (d for d in itertools.product((-1, 0, 1), repeat=3) if d != (0, 0, 0)),
        key=lambda d: (-abs(d[2]), -abs(d[0]) - abs(d[1])),
    )
)
OWN_CELLS = tuple(itertools.product(range(2), repeat=3))
CHUNKS = 8
KINDS = 96


def place(d):
    return ((d[0] + 1) * 3 + d[1] + 1) * 3 + d[2] + 1


def chunk_of(d):
    return abs(d[0]) * 4 + abs(d[1]) * 2 + abs(d[2])


def dot(a, b, ca, cb):
    return lax.dot_general(a, b, (((ca,), (cb,)), ((), ())), preferred_element_type=F32)


def nn(a, b):
    return dot(a, b, 1, 0)


def tn(a, b):
    return dot(a, b, 0, 0)


def nt(a, b):
    return dot(a, b, 1, 1)


def rows_iota(shape):
    return lax.broadcasted_iota(jnp.int32, shape, 0)


def lanes_iota(shape):
    return lax.broadcasted_iota(jnp.int32, shape, 1)


def mask(condition):
    return jnp.where(condition, 1.0, 0.0).astype(BF16)


def hot(rows, wanted):
    return jnp.where(tile(rows) == wanted.astype(F32).astype(BF16), BF16(1), BF16(0))


def fold(x):
    total = x[:, :ATOMS]
    for r in range(1, DEG):
        total = total + x[:, r * ATOMS : (r + 1) * ATOMS]
    return total


def tile(x):
    return jnp.concatenate([x] * DEG, axis=1)


def silu_of_half(half):
    up = 1.0 + jnp.tanh(half)
    value = (half * up).astype(BF16)
    gate = BF16(0.5) * up.astype(BF16)
    return value, gate + value * (BF16(1) - gate)


def silu(x):
    half = 0.5 * x
    up = 1.0 + jnp.tanh(half)
    value = half * up
    gate = 0.5 * up
    return value, gate + value * (1.0 - gate)


def in_turns(several, depth):
    waiting, active = list(several), []
    while waiting or active:
        if waiting and len(active) < depth:
            active.append(waiting.pop(0))
        for steps in tuple(active):
            if next(steps, True):
                active.remove(steps)


def two(x):
    high = x.astype(BF16)
    return high, (x - high.astype(F32)).astype(BF16)


def kernel(
    sizes,
    off,
    spe,
    cnt,
    edg,
    emb,
    rin,
    rhid,
    rout,
    mix1,
    proj,
    mix2,
    rdo,
    frc,
    eng,
    vm,
    in_sem,
    blk,
    sel,
    geo,
    srt,
    embp,
    bas,
    rls,
    nqs,
    ohot,
    vec,
    rad2,
    act,
    act2,
    usrc,
    scl,
    gt,
    gtt,
    lg,
    dl,
    gsum,
    drs,
    numbered,
    by_four,
    tgs,
    pgs,
    pgx,
    pr,
    esx,
    esy,
    esz,
    geo_s,
    geo_r,
    pos_s,
    pos_r,
    en_s,
    en_r,
):
    me = tuple(lax.axis_index(a) for a in AXES)
    incoming = (off, spe, cnt, edg, emb, rin, rhid, rout, mix1, proj, mix2, rdo)
    loads = []
    for i, (src, dst) in enumerate(zip(incoming, vm)):
        loads.append(pltpu.make_async_copy(src, dst, in_sem.at[i]))
    for i in (3, 0, 1, 2, 4, 5, 6, 7, 8, 9, 10, 11):
        loads[i].start()
    off, spe, cnt, edg, emb, rin, rhid, rout, mix1, proj, mix2, rdo = vm

    def at(offset):
        return tuple(lax.rem(m + d + n, n) for m, d, n in zip(me, offset, sizes))

    def remote(src, dst, send, recv, offset):
        return pltpu.make_async_remote_copy(
            src_ref=src,
            dst_ref=dst,
            send_sem=send,
            recv_sem=recv,
            device_id=at(offset),
            device_id_type=MESH,
        )

    def axis_offset(axis, d):
        return tuple(d if k == axis else 0 for k in range(3))

    greeted = list(NEIGHBOURS)
    for axis, n in enumerate(sizes):
        greeted += [axis_offset(axis, d) for d in range(2, n - 1)]
    barrier = pltpu.get_barrier_semaphore()
    for d in greeted:
        pl.semaphore_signal(barrier, inc=1, device_id=at(d), device_id_type=MESH)

    loads[3].wait()
    target = edg[0, 0, 0]
    source = edg[1, 0, 0]
    chosen = mask(rows_iota((ATOMS, EDGES)) == target)
    lane2 = lanes_iota((ATOMS, 2 * ATOMS))
    before = mask((rows_iota((ATOMS, 2 * ATOMS)) < lane2) | (lane2 >= ATOMS))
    high_part = (source >> 3).astype(F32)
    low_part = (source & 7).astype(F32)
    base = jnp.zeros((ATOMS, ATOMS), F32)
    table = jnp.zeros((24, ATOMS), F32)
    for b in range(DEG):
        cut = slice(b * ATOMS, (b + 1) * ATOMS)
        part = chosen[:, cut]
        counted = nn(part, before)
        rank = jnp.sum((counted[:, :ATOMS] + base) * part.astype(F32), axis=0, keepdims=True)
        base = base + counted[:, ATOMS:]
        placed = jnp.where(rows_iota((DEG, ATOMS)).astype(F32) == rank, 1.0, 0.0)
        stacked = jnp.concatenate(
            [placed * high_part[:, cut], placed * low_part[:, cut], placed], axis=0
        ).astype(BF16)
        table = table + nt(stacked, part)
    found = table[0:8] * 8.0 + table[8:16] + table[16:24]
    mine = place((0, 0, 0))
    blk[mine, 0:4, :] = found[0:4] * 2048.0 + found[4:8]

    loads[0].wait()
    loads[1].wait()
    for i, (x, y, z) in enumerate(OWN_CELLS):
        here = slice(i * 16, i * 16 + 16)
        for k in range(3):
            blk[mine, 4 + k : 5 + k, here] = off[k, x, y, z : z + 1, :]
        blk[mine, 7:8, here] = spe[x, y, z : z + 1, :].astype(F32)

    pl.semaphore_wait(barrier, len(greeted))
    pending = []
    geo_copies = []
    for i, d in enumerate(NEIGHBOURS):
        there = place(tuple(-k for k in d))
        copy = remote(blk.at[mine], blk.at[there], geo_s.at[i], geo_r.at[i], d)
        copy.start()
        geo_copies.append(copy)
    pending += geo_copies

    for i in (2, 4, 5, 6, 7, 8, 9, 10, 11):
        loads[i].wait()
    half_in = [(0.5 * rin[k].astype(F32)).astype(BF16) for k in range(2)]
    half_hid = [(0.5 * rhid[k].astype(F32)).astype(BF16) for k in range(2)]
    joined = nn(mix1[1], proj[1]).astype(BF16)
    embp[...] = jnp.zeros((KINDS, C), F32)
    embp[0:89, :] = emb[...].astype(F32)
    geo[...] = jnp.zeros((112, ATOMS), F32)
    adds = mask((lanes_iota((8, 3 * C)) >> 7) == rows_iota((8, 3 * C)))
    numbered[...] = rows_iota((ATOMS, ATOMS)).astype(F32).astype(BF16)
    by_four[...] = (rows_iota((112, ATOMS)) >> 2).astype(F32).astype(BF16)
    widths = jnp.zeros((8, EDGES), F32)
    for k in range(8):
        widths = jnp.where(rows_iota((8, EDGES)) == k, WIDTHS[k], widths)
    own_lane = lanes_iota((1, ATOMS))
    own_cell = (own_lane >> 6, (own_lane >> 5) & 1, (own_lane >> 4) & 1)
    readout = jnp.broadcast_to(rdo[...].reshape(1, C), (C, C)).T
    occupied = jnp.zeros((1, ATOMS), F32)
    for i, (x, y, z) in enumerate(OWN_CELLS):
        here = ((own_lane >> 4) == i) & ((own_lane & 15) < cnt[x, y, z])
        occupied = jnp.where(here, 1.0, occupied)
    weight = readout * occupied

    source_row = found.astype(jnp.int32) - 1
    srt[0] = source_row
    cell = source_row >> 4
    near = (cell >> 4, (cell >> 2) & 3, cell & 3)
    chunk = jnp.zeros((DEG, ATOMS), jnp.int32)
    atom = jnp.zeros((DEG, ATOMS), jnp.int32)
    for p in near:
        chunk = chunk * 2 + 1 - (((p + 1) >> 1) & 1)
        atom = atom * 2 + ((p + 1) & 1)
    row = jnp.where(source_row >= 0, chunk * ATOMS + atom * 16 + (source_row & 15), -1)
    srt[1] = row
    column = row.astype(F32).T
    for r in range(DEG):
        cut = slice(r * ATOMS, (r + 1) * ATOMS)
        gt[:, cut] = mask(rows_iota((1024, ATOMS)) == srt[1, r : r + 1, :])
        at_lane = lanes_iota((ATOMS, 1024)).astype(F32)
        gtt[cut, :] = mask(at_lane == column[:, r : r + 1])

    def lanes_of(d):
        chosen = own_lane >= 0
        for step, cell in zip(d, own_cell):
            if step:
                chosen = chosen & (cell == (0 if step > 0 else 1))
        return chosen

    for copy in geo_copies:
        copy.wait_recv()
    gathered_blocks = [jnp.zeros((8, ATOMS), F32)] * CHUNKS
    for d in itertools.product((-1, 0, 1), repeat=3):
        n = place(d)
        block = blk[n]
        geo[n * 4 : n * 4 + 4, :] = block[4:8]
        a = chunk_of(d)
        gathered_blocks[a] = jnp.where(lanes_of(d), block, gathered_blocks[a])
    for a in range(CHUNKS):
        sel[a] = gathered_blocks[a]
        if a:
            packed = gathered_blocks[a][0:4].astype(jnp.int32)
            srt[a] = jnp.concatenate([packed >> 11, packed & 2047], axis=0) - 1
    places = jnp.concatenate(two(geo[...]), axis=1)

    def radial(weights, basis_low, act):
        first = tn(half_in[weights], basis_low)
        yield
        first, slope = silu_of_half(first)
        act[0] = slope
        second = tn(half_hid[weights], first)
        yield
        second, slope = silu_of_half(second)
        act[1] = slope
        out = tn(rout[weights], second)
        yield
        return out

    def radial_back(weights, grad, basis, act):
        back = nn(rout[weights], grad)
        yield
        back = nn(rhid[weights], back.astype(BF16) * act[1])
        yield
        back = nn(rin[weights], back.astype(BF16) * act[0])
        yield
        return -2.0 * jnp.sum(back * widths * basis, axis=0, keepdims=True)

    def forward(a):
        far = (a >> 2, (a >> 1) & 1, a & 1)
        srow = jnp.concatenate([srt[a, r : r + 1, :] for r in range(DEG)], axis=1)
        cell = srow >> 4
        near = (cell >> 4, (cell >> 2) & 3, cell & 3)
        cells = [(p + 1) & 1 for p in near]
        atom = ((cells[0] * 2 + cells[1]) * 2 + cells[2]) * 16 + (srow & 15)
        device = jnp.zeros((1, EDGES), jnp.int32)
        for p, f, own in zip(near, far, own_cell):
            device = device * 3 + ((p + 1) >> 1) + tile(f * (1 - 2 * own))
        device = jnp.where(srow >= 0, device, -1)
        onehot = hot(numbered[...], atom)
        ohot[a] = onehot
        found = nn(places, jnp.concatenate([onehot, onehot], axis=0))
        yield
        nqs[a] = hot(by_four[...], device)
        found = jnp.where((rows_iota((112, EDGES)) >> 2) == device, found, 0.0)
        total = found[0:8]
        for i in range(1, 14):
            total = total + found[i * 8 : i * 8 + 8]
        total = total[0:4] + total[4:8]
        rel = []
        for k in range(3):
            step = (near[k] - 1 - tile(own_cell[k])).astype(F32)
            rel.append(step + (total[k : k + 1] - tile(sel[a, 4 + k : 5 + k, :])) / CELL)
            rls[a, k : k + 1, :] = rel[k]
        squared = rel[0] * rel[0] + rel[1] * rel[1] + rel[2] * rel[2]
        basis = jnp.exp(-squared * widths)
        bas[a] = basis
        weights = yield from radial(0, basis.astype(BF16), act.at[a])
        kinds = jnp.where(srow >= 0, total[3:4].astype(jnp.int32), -1)
        kept = tn(embp[...].astype(BF16), hot(numbered[0:KINDS, :], kinds))
        usrc[a] = kept.astype(BF16)
        where = slice(a * ATOMS, (a + 1) * ATOMS)
        scl[0:C, where] = (fold(weights[:C] * kept) * RSQRT).astype(BF16)
        vector = weights[C:] * kept
        vec[a] = vector.astype(BF16)
        for k in range(3):
            scl[(k + 1) * C : (k + 2) * C, where] = (fold(vector * rel[k]) * RSQRT).astype(BF16)

    def weights_two():
        rad2[...] = yield from radial(1, bas[0].astype(BF16), act2)

    in_turns([forward(a) for a in range(CHUNKS)] + [weights_two()], 3)

    scalars, mixed_slope = silu(tn(mix1[0], scl[:C]))
    lifted = [tn(proj[0], scalars.astype(BF16)).astype(BF16)]
    lifted += [tn(joined, scl[k * C : (k + 1) * C]).astype(BF16) for k in range(1, 4)]

    rel = [rls[0, k : k + 1, :] for k in range(3)]
    lg[...] = nn(jnp.concatenate(lifted, axis=0), gt[...])
    inner_sum = rel[0] * lg[C : 2 * C] + rel[1] * lg[2 * C : 3 * C] + rel[2] * lg[3 * C :]
    summed_two = fold(rad2[:C] * lg[:C] + rad2[C:] * inner_sum)
    rows = tn(mix2[...], (summed_two * RSQRT).astype(BF16)) + scalars[:, :ATOMS]
    energy, slope = silu(rows)
    local = jnp.sum(energy * weight, axis=0, keepdims=True)
    local = jnp.sum(local, axis=1, keepdims=True)
    grad_rows = weight * slope
    grad = tile(nn(mix2[...], grad_rows.astype(BF16)) * RSQRT)

    def share(axis, buffer, value, first):
        buffer[me[axis]] = jnp.broadcast_to(value, (1, ATOMS))
        copies = []
        for d in range(1, sizes[axis]):
            here = buffer.at[me[axis]]
            copy = remote(
                here, here, en_s.at[first + d - 1], en_r.at[first + d - 1], axis_offset(axis, d)
            )
            copy.start()
            copies.append(copy)
        pending.extend(copies)
        return copies

    def gathered(axis, buffer, copies):
        for copy in copies:
            copy.wait_recv()
        total = buffer[0]
        for i in range(1, sizes[axis]):
            total = total + buffer[i]
        return total[:, 0:1]

    e_copies = share(2, esz, local, sizes[0] + sizes[1])

    grad_inner = grad * rad2[C:]
    dl[:C] = (grad * rad2[:C]).astype(BF16)
    for k in range(3):
        dl[(k + 1) * C : (k + 2) * C] = (grad_inner * rel[k]).astype(BF16)
    back = nn(dl[...], gtt[...]).astype(BF16)

    def backward_two():
        pull = yield from radial_back(
            1, jnp.concatenate([grad * lg[:C], grad * inner_sum], axis=0).astype(BF16), bas[0], act2
        )
        for k in range(3):
            direct = jnp.sum(grad_inner * lg[(k + 1) * C : (k + 2) * C], axis=0, keepdims=True)
            drs[k : k + 1, :] = rel[k] * pull + direct

    own_rows = jnp.concatenate([grad_rows, jnp.zeros((C, 1024 - ATOMS), F32)], axis=1)
    grad_mixed = (nn(proj[0], back[:C]) + own_rows) * mixed_slope
    gsum[:C] = (nn(mix1[0], grad_mixed.astype(BF16)) * RSQRT).astype(BF16)
    for k in range(1, 4):
        cut = slice(k * C, (k + 1) * C)
        gsum[cut] = (nn(joined, back[cut]) * RSQRT).astype(BF16)

    def backward(a):
        where = slice(a * ATOMS, (a + 1) * ATOMS)
        grads = [tile(gsum[k * C : (k + 1) * C, where]) for k in range(4)]
        rel = [rls[a, k : k + 1, :] for k in range(3)]
        low = [r.astype(BF16) for r in rel]
        towards = low[0] * grads[1] + low[1] * grads[2] + low[2] * grads[3]
        kept = usrc[a]
        pull = yield from radial_back(
            0,
            jnp.concatenate([grads[0] * kept, towards * kept], axis=0),
            bas[a],
            act.at[a],
        )
        vector = vec[a]
        direct = nn(adds, jnp.concatenate([vector * g for g in grads[1:]], axis=0))
        moved = []
        for k in range(3):
            pulled = rel[k] * pull + direct[k : k + 1]
            if a == 0:
                pulled = pulled + drs[k : k + 1, :]
            moved.append(pulled / CELL)
            tgs[a, k : k + 1, :] = fold(moved[k])
        moved.append(jnp.zeros((1, EDGES), F32))
        moved = jnp.concatenate(moved * 4, axis=0).astype(BF16)
        spread = jnp.concatenate([moved] * 7, axis=0) * nqs[a]
        spreads.append(nt(spread, ohot[a]))

    tgs[...] = jnp.zeros((CHUNKS, 4, ATOMS), F32)
    spreads = []
    in_turns([backward_two()] + [backward(a) for a in (1, 2, 3, 4, 5, 6, 7, 0)], 3)
    pgs[...] = sum(spreads)

    pos_copies = []
    for d in itertools.product((-1, 0, 1), repeat=3):
        n = place(d)
        pgx[n] = pgs[n * 4 : n * 4 + 4, :] - jnp.where(lanes_of(d), tgs[chunk_of(d)], 0.0)
    for i, d in enumerate(NEIGHBOURS):
        there = place(tuple(-k for k in d))
        copy = remote(
            pgx.at[place(d), 0:3], pr.at[there, 0:3], pos_s.at[i], pos_r.at[i], d
        )
        copy.start()
        pos_copies.append(copy)
    pending += pos_copies
    e_copies = share(1, esy, gathered(2, esz, e_copies), sizes[0])
    e_copies = share(0, esx, gathered(1, esy, e_copies), 0)
    for copy in pos_copies:
        copy.wait_recv()
    total = pgx[mine, 0:3, :]
    for d in NEIGHBOURS:
        total = total + pr[place(d), 0:3, :]
    for i, (x, y, z) in enumerate(OWN_CELLS):
        for k in range(3):
            frc[k, x, y, z : z + 1, :] = -total[k : k + 1, i * 16 : i * 16 + 16]
    eng[...] = gathered(0, esx, e_copies) / float(ATOMS * sizes[0] * sizes[1] * sizes[2])
    for copy in pending:
        copy.wait_send()


def body(sizes, *args):
    hbm = pl.BlockSpec(memory_space=pltpu.HBM)
    vmem = pl.BlockSpec(memory_space=pltpu.VMEM)
    held = [pltpu.VMEM(a.shape, a.dtype) for a in args]
    held[2] = pltpu.SMEM(args[2].shape, args[2].dtype)
    energy_sends = sum(sizes)
    dma = pltpu.SemaphoreType.DMA
    scratch = [
        tuple(held),
        dma((len(args),)),
        pltpu.VMEM((27, 8, 128), F32),
        pltpu.VMEM((8, 8, 128), F32),
        pltpu.VMEM((112, 128), F32),
        pltpu.VMEM((8, 8, 128), jnp.int32),
        pltpu.VMEM((96, 128), F32),
        pltpu.VMEM((8, 8, 1024), F32),
        pltpu.VMEM((8, 3, 1024), F32),
        pltpu.VMEM((8, 112, 1024), BF16),
        pltpu.VMEM((8, 128, 1024), BF16),
        pltpu.VMEM((8, 128, 1024), BF16),
        pltpu.VMEM((256, 1024), F32),
        pltpu.VMEM((8, 2, 64, 1024), BF16),
        pltpu.VMEM((2, 64, 1024), BF16),
        pltpu.VMEM((8, 128, 1024), BF16),
        pltpu.VMEM((512, 1024), BF16),
        pltpu.VMEM((1024, 1024), BF16),
        pltpu.VMEM((1024, 1024), BF16),
        pltpu.VMEM((512, 1024), F32),
        pltpu.VMEM((512, 1024), BF16),
        pltpu.VMEM((512, 1024), BF16),
        pltpu.VMEM((8, 1024), F32),
        pltpu.VMEM((128, 128), BF16),
        pltpu.VMEM((112, 128), BF16),
        pltpu.VMEM((8, 4, 128), F32),
        pltpu.VMEM((112, 128), F32),
        pltpu.VMEM((27, 4, 128), F32),
        pltpu.VMEM((27, 4, 128), F32),
        pltpu.VMEM((sizes[0], 1, 128), F32),
        pltpu.VMEM((sizes[1], 1, 128), F32),
        pltpu.VMEM((sizes[2], 1, 128), F32),
        dma((26,)),
        dma((26,)),
        dma((26,)),
        dma((26,)),
        dma((energy_sends,)),
        dma((energy_sends,)),
    ]
    forces, energy = pl.pallas_call(
        functools.partial(kernel, sizes),
        out_shape=(
            jax.ShapeDtypeStruct(args[0].shape, F32),
            jax.ShapeDtypeStruct((1, 1), F32),
        ),
        in_specs=[hbm] * len(args),
        out_specs=(vmem, vmem),
        scratch_shapes=scratch,
        compiler_params=pltpu.CompilerParams(
            collective_id=0, has_side_effects=True, vmem_limit_bytes=62 * 1024 * 1024
        ),
    )(*args)
    return forces, energy.reshape(())


def solution(mesh):
    sizes = tuple(mesh.shape[a] for a in AXES)
    in_specs = (
        P(None, "gx", "gy", "gz", None),
        P("gx", "gy", "gz", None),
        P("gx", "gy", "gz"),
        P(None, "gx", "gy", "gz", None),
    ) + (P(),) * 8
    out_specs = (P(None, "gx", "gy", "gz", None), P())
    return jax.shard_map(
        functools.partial(body, sizes),
        mesh=mesh,
        in_specs=in_specs,
        out_specs=out_specs,
        check_vma=False,
    )
```

```python
import functools
import itertools

import jax
import jax.numpy as jnp
from jax import lax
from jax.experimental import pallas as pl
from jax.experimental.pallas import tpu as pltpu
from jax.sharding import PartitionSpec as P

F32 = jnp.float32
BF16 = jnp.bfloat16
MESH = pl.DeviceIdType.MESH
AXES = ("gx", "gy", "gz")

C = 128
CELL = 6.0
DEG = 8
ATOMS = 128
EDGES = 1024
WIDTHS = tuple(0.1 * 30.0 ** (k / 7) for k in range(8))
RSQRT = 1.0 / DEG**0.5

NEIGHBOURS = tuple(
    sorted(
        (d for d in itertools.product((-1, 0, 1), repeat=3) if d != (0, 0, 0)),
        key=lambda d: (-abs(d[2]), -abs(d[0]) - abs(d[1])),
    )
)
OWN_CELLS = tuple(itertools.product(range(2), repeat=3))
CHUNKS = 8
KINDS = 96


def place(d):
    return ((d[0] + 1) * 3 + d[1] + 1) * 3 + d[2] + 1


def chunk_of(d):
    return abs(d[0]) * 4 + abs(d[1]) * 2 + abs(d[2])


def dot(a, b, ca, cb):
    return lax.dot_general(a, b, (((ca,), (cb,)), ((), ())), preferred_element_type=F32)


def nn(a, b):
    return dot(a, b, 1, 0)


def tn(a, b):
    return dot(a, b, 0, 0)


def nt(a, b):
    return dot(a, b, 1, 1)


def rows_iota(shape):
    return lax.broadcasted_iota(jnp.int32, shape, 0)


def lanes_iota(shape):
    return lax.broadcasted_iota(jnp.int32, shape, 1)


def mask(condition):
    return jnp.where(condition, 1.0, 0.0).astype(BF16)


def hot(rows, wanted):
    return jnp.where(tile(rows) == wanted.astype(F32).astype(BF16), BF16(1), BF16(0))


def fold(x):
    total = x[:, :ATOMS]
    for r in range(1, DEG):
        total = total + x[:, r * ATOMS : (r + 1) * ATOMS]
    return total


def tile(x):
    return jnp.concatenate([x] * DEG, axis=1)


def silu_of_half(half):
    up = 1.0 + jnp.tanh(half)
    value = (half * up).astype(BF16)
    gate = BF16(0.5) * up.astype(BF16)
    return value, gate + value * (BF16(1) - gate)


def silu(x):
    half = 0.5 * x
    up = 1.0 + jnp.tanh(half)
    value = half * up
    gate = 0.5 * up
    return value, gate + value * (1.0 - gate)


def in_turns(several, depth):
    waiting, active = list(several), []
    while waiting or active:
        if waiting and len(active) < depth:
            active.append(waiting.pop(0))
        for steps in tuple(active):
            if next(steps, True):
                active.remove(steps)


def two(x):
    high = x.astype(BF16)
    return high, (x - high.astype(F32)).astype(BF16)


def kernel(
    sizes,
    off,
    spe,
    cnt,
    edg,
    emb,
    rin,
    rhid,
    rout,
    mix1,
    proj,
    mix2,
    rdo,
    frc,
    eng,
    vm,
    in_sem,
    blk,
    sel,
    geo,
    srt,
    embp,
    bas,
    rls,
    nqs,
    ohot,
    vec,
    rad2,
    act,
    act2,
    usrc,
    scl,
    gt,
    gtt,
    lg,
    dl,
    gsum,
    drs,
    numbered,
    by_four,
    tgs,
    pgs,
    pgx,
    pr,
    esx,
    esy,
    esz,
    geo_s,
    geo_r,
    pos_s,
    pos_r,
    en_s,
    en_r,
):
    me = tuple(lax.axis_index(a) for a in AXES)
    incoming = (off, spe, cnt, edg, emb, rin, rhid, rout, mix1, proj, mix2, rdo)
    loads = []
    for i, (src, dst) in enumerate(zip(incoming, vm)):
        loads.append(pltpu.make_async_copy(src, dst, in_sem.at[i]))
    for i in (3, 0, 1, 2, 4, 5, 6, 7, 8, 9, 10, 11):
        loads[i].start()
    off, spe, cnt, edg, emb, rin, rhid, rout, mix1, proj, mix2, rdo = vm

    def at(offset):
        return tuple(lax.rem(m + d + n, n) for m, d, n in zip(me, offset, sizes))

    def remote(src, dst, send, recv, offset):
        return pltpu.make_async_remote_copy(
            src_ref=src,
            dst_ref=dst,
            send_sem=send,
            recv_sem=recv,
            device_id=at(offset),
            device_id_type=MESH,
        )

    def axis_offset(axis, d):
        return tuple(d if k == axis else 0 for k in range(3))

    greeted = list(NEIGHBOURS)
    for axis, n in enumerate(sizes):
        greeted += [axis_offset(axis, d) for d in range(2, n - 1)]
    barrier = pltpu.get_barrier_semaphore()
    for d in greeted:
        pl.semaphore_signal(barrier, inc=1, device_id=at(d), device_id_type=MESH)

    loads[3].wait()
    target = edg[0, 0, 0]
    source = edg[1, 0, 0]
    chosen = mask(rows_iota((ATOMS, EDGES)) == target)
    lane2 = lanes_iota((ATOMS, 2 * ATOMS))
    before = mask((rows_iota((ATOMS, 2 * ATOMS)) < lane2) | (lane2 >= ATOMS))
    high_part = (source >> 3).astype(F32)
    low_part = (source & 7).astype(F32)
    base = jnp.zeros((ATOMS, ATOMS), F32)
    table = jnp.zeros((24, ATOMS), F32)
    for b in range(DEG):
        cut = slice(b * ATOMS, (b + 1) * ATOMS)
        part = chosen[:, cut]
        counted = nn(part, before)
        rank = jnp.sum((counted[:, :ATOMS] + base) * part.astype(F32), axis=0, keepdims=True)
        base = base + counted[:, ATOMS:]
        placed = jnp.where(rows_iota((DEG, ATOMS)).astype(F32) == rank, 1.0, 0.0)
        stacked = jnp.concatenate(
            [placed * high_part[:, cut], placed * low_part[:, cut], placed], axis=0
        ).astype(BF16)
        table = table + nt(stacked, part)
    found = table[0:8] * 8.0 + table[8:16] + table[16:24]
    mine = place((0, 0, 0))
    blk[mine, 0:4, :] = found[0:4] * 2048.0 + found[4:8]

    loads[0].wait()
    loads[1].wait()
    for i, (x, y, z) in enumerate(OWN_CELLS):
        here = slice(i * 16, i * 16 + 16)
        for k in range(3):
            blk[mine, 4 + k : 5 + k, here] = off[k, x, y, z : z + 1, :]
        blk[mine, 7:8, here] = spe[x, y, z : z + 1, :].astype(F32)

    pl.semaphore_wait(barrier, len(greeted))
    pending = []
    geo_copies = []
    for i, d in enumerate(NEIGHBOURS):
        there = place(tuple(-k for k in d))
        copy = remote(blk.at[mine], blk.at[there], geo_s.at[i], geo_r.at[i], d)
        copy.start()
        geo_copies.append(copy)
    pending += geo_copies

    for i in (2, 4, 5, 6, 7, 8, 9, 10, 11):
        loads[i].wait()
    half_in = [(0.5 * rin[k].astype(F32)).astype(BF16) for k in range(2)]
    half_hid = [(0.5 * rhid[k].astype(F32)).astype(BF16) for k in range(2)]
    joined = nn(mix1[1], proj[1]).astype(BF16)
    embp[...] = jnp.zeros((KINDS, C), F32)
    embp[0:89, :] = emb[...].astype(F32)
    geo[...] = jnp.zeros((112, ATOMS), F32)
    adds = mask((lanes_iota((8, 3 * C)) >> 7) == rows_iota((8, 3 * C)))
    numbered[...] = rows_iota((ATOMS, ATOMS)).astype(F32).astype(BF16)
    by_four[...] = (rows_iota((112, ATOMS)) >> 2).astype(F32).astype(BF16)
    widths = jnp.zeros((8, EDGES), F32)
    for k in range(8):
        widths = jnp.where(rows_iota((8, EDGES)) == k, WIDTHS[k], widths)
    own_lane = lanes_iota((1, ATOMS))
    own_cell = (own_lane >> 6, (own_lane >> 5) & 1, (own_lane >> 4) & 1)
    readout = jnp.broadcast_to(rdo[...].reshape(1, C), (C, C)).T
    occupied = jnp.zeros((1, ATOMS), F32)
    for i, (x, y, z) in enumerate(OWN_CELLS):
        here = ((own_lane >> 4) == i) & ((own_lane & 15) < cnt[x, y, z])
        occupied = jnp.where(here, 1.0, occupied)
    weight = readout * occupied

    source_row = found.astype(jnp.int32) - 1
    srt[0] = source_row
    cell = source_row >> 4
    near = (cell >> 4, (cell >> 2) & 3, cell & 3)
    chunk = jnp.zeros((DEG, ATOMS), jnp.int32)
    atom = jnp.zeros((DEG, ATOMS), jnp.int32)
    for p in near:
        chunk = chunk * 2 + 1 - (((p + 1) >> 1) & 1)
        atom = atom * 2 + ((p + 1) & 1)
    row = jnp.where(source_row >= 0, chunk * ATOMS + atom * 16 + (source_row & 15), -1)
    srt[1] = row
    column = row.astype(F32).T
    for r in range(DEG):
        cut = slice(r * ATOMS, (r + 1) * ATOMS)
        gt[:, cut] = mask(rows_iota((1024, ATOMS)) == srt[1, r : r + 1, :])
        at_lane = lanes_iota((ATOMS, 1024)).astype(F32)
        gtt[cut, :] = mask(at_lane == column[:, r : r + 1])

    def lanes_of(d):
        chosen = own_lane >= 0
        for step, cell in zip(d, own_cell):
            if step:
                chosen = chosen & (cell == (0 if step > 0 else 1))
        return chosen

    for copy in geo_copies:
        copy.wait_recv()
    gathered_blocks = [jnp.zeros((8, ATOMS), F32)] * CHUNKS
    for d in itertools.product((-1, 0, 1), repeat=3):
        n = place(d)
        block = blk[n]
        geo[n * 4 : n * 4 + 4, :] = block[4:8]
        a = chunk_of(d)
        gathered_blocks[a] = jnp.where(lanes_of(d), block, gathered_blocks[a])
    for a in range(CHUNKS):
        sel[a] = gathered_blocks[a]
        if a:
            packed = gathered_blocks[a][0:4].astype(jnp.int32)
            srt[a] = jnp.concatenate([packed >> 11, packed & 2047], axis=0) - 1
    places = jnp.concatenate(two(geo[...]), axis=1)

    def radial(weights, basis_low, act):
        first = tn(half_in[weights], basis_low)
        yield
        first, slope = silu_of_half(first)
        act[0] = slope
        second = tn(half_hid[weights], first)
        yield
        second, slope = silu_of_half(second)
        act[1] = slope
        out = tn(rout[weights], second)
        yield
        return out

    def radial_back(weights, grad, basis, act):
        back = nn(rout[weights], grad)
        yield
        back = nn(rhid[weights], back.astype(BF16) * act[1])
        yield
        back = nn(rin[weights], back.astype(BF16) * act[0])
        yield
        return -2.0 * jnp.sum(back * widths * basis, axis=0, keepdims=True)

    def forward(a):
        far = (a >> 2, (a >> 1) & 1, a & 1)
        srow = jnp.concatenate([srt[a, r : r + 1, :] for r in range(DEG)], axis=1)
        cell = srow >> 4
        near = (cell >> 4, (cell >> 2) & 3, cell & 3)
        cells = [(p + 1) & 1 for p in near]
        atom = ((cells[0] * 2 + cells[1]) * 2 + cells[2]) * 16 + (srow & 15)
        device = jnp.zeros((1, EDGES), jnp.int32)
        for p, f, own in zip(near, far, own_cell):
            device = device * 3 + ((p + 1) >> 1) + tile(f * (1 - 2 * own))
        device = jnp.where(srow >= 0, device, -1)
        onehot = hot(numbered[...], atom)
        ohot[a] = onehot
        found = nn(places, jnp.concatenate([onehot, onehot], axis=0))
        yield
        nqs[a] = hot(by_four[...], device)
        found = jnp.where((rows_iota((112, EDGES)) >> 2) == device, found, 0.0)
        total = found[0:8]
        for i in range(1, 14):
            total = total + found[i * 8 : i * 8 + 8]
        total = total[0:4] + total[4:8]
        rel = []
        for k in range(3):
            step = (near[k] - 1 - tile(own_cell[k])).astype(F32)
            rel.append(step + (total[k : k + 1] - tile(sel[a, 4 + k : 5 + k, :])) / CELL)
            rls[a, k : k + 1, :] = rel[k]
        squared = rel[0] * rel[0] + rel[1] * rel[1] + rel[2] * rel[2]
        basis = jnp.exp(-squared * widths)
        bas[a] = basis
        weights = yield from radial(0, basis.astype(BF16), act.at[a])
        kinds = jnp.where(srow >= 0, total[3:4].astype(jnp.int32), -1)
        kept = tn(embp[...].astype(BF16), hot(numbered[0:KINDS, :], kinds))
        usrc[a] = kept.astype(BF16)
        where = slice(a * ATOMS, (a + 1) * ATOMS)
        scl[0:C, where] = (fold(weights[:C] * kept) * RSQRT).astype(BF16)
        vector = weights[C:] * kept
        vec[a] = vector.astype(BF16)
        for k in range(3):
            scl[(k + 1) * C : (k + 2) * C, where] = (fold(vector * rel[k]) * RSQRT).astype(BF16)

    def weights_two():
        rad2[...] = yield from radial(1, bas[0].astype(BF16), act2)

    in_turns([forward(a) for a in range(CHUNKS)] + [weights_two()], 3)

    scalars, mixed_slope = silu(tn(mix1[0], scl[:C]))
    lifted = [tn(proj[0], scalars.astype(BF16)).astype(BF16)]
    lifted += [tn(joined, scl[k * C : (k + 1) * C]).astype(BF16) for k in range(1, 4)]

    rel = [rls[0, k : k + 1, :] for k in range(3)]
    lg[...] = nn(jnp.concatenate(lifted, axis=0), gt[...])
    inner_sum = rel[0] * lg[C : 2 * C] + rel[1] * lg[2 * C : 3 * C] + rel[2] * lg[3 * C :]
    summed_two = fold(rad2[:C] * lg[:C] + rad2[C:] * inner_sum)
    rows = tn(mix2[...], (summed_two * RSQRT).astype(BF16)) + scalars[:, :ATOMS]
    energy, slope = silu(rows)
    local = jnp.sum(energy * weight, axis=0, keepdims=True)
    local = jnp.sum(local, axis=1, keepdims=True)
    grad_rows = weight * slope
    grad = tile(nn(mix2[...], grad_rows.astype(BF16)) * RSQRT)

    def share(axis, buffer, value, first):
        buffer[me[axis]] = jnp.broadcast_to(value, (1, ATOMS))
        copies = []
        for d in range(1, sizes[axis]):
            here = buffer.at[me[axis]]
            copy = remote(
                here, here, en_s.at[first + d - 1], en_r.at[first + d - 1], axis_offset(axis, d)
            )
            copy.start()
            copies.append(copy)
        pending.extend(copies)
        return copies

    def gathered(axis, buffer, copies):
        for copy in copies:
            copy.wait_recv()
        total = buffer[0]
        for i in range(1, sizes[axis]):
            total = total + buffer[i]
        return total[:, 0:1]

    e_copies = share(2, esz, local, sizes[0] + sizes[1])

    grad_inner = grad * rad2[C:]
    dl[:C] = (grad * rad2[:C]).astype(BF16)
    for k in range(3):
        dl[(k + 1) * C : (k + 2) * C] = (grad_inner * rel[k]).astype(BF16)
    back = nn(dl[...], gtt[...]).astype(BF16)

    def backward_two():
        pull = yield from radial_back(
            1, jnp.concatenate([grad * lg[:C], grad * inner_sum], axis=0).astype(BF16), bas[0], act2
        )
        parts = [(grad_inner * lg[(k + 1) * C : (k + 2) * C]).astype(BF16) for k in range(3)]
        direct = nn(adds, jnp.concatenate(parts, axis=0))
        for k in range(3):
            drs[k : k + 1, :] = rel[k] * pull + direct[k : k + 1]

    own_rows = jnp.concatenate([grad_rows, jnp.zeros((C, 1024 - ATOMS), F32)], axis=1)
    grad_mixed = (nn(proj[0], back[:C]) + own_rows) * mixed_slope
    gsum[:C] = (nn(mix1[0], grad_mixed.astype(BF16)) * RSQRT).astype(BF16)
    for k in range(1, 4):
        cut = slice(k * C, (k + 1) * C)
        gsum[cut] = (nn(joined, back[cut]) * RSQRT).astype(BF16)

    def backward(a):
        where = slice(a * ATOMS, (a + 1) * ATOMS)
        grads = [tile(gsum[k * C : (k + 1) * C, where]) for k in range(4)]
        rel = [rls[a, k : k + 1, :] for k in range(3)]
        low = [r.astype(BF16) for r in rel]
        towards = low[0] * grads[1] + low[1] * grads[2] + low[2] * grads[3]
        kept = usrc[a]
        pull = yield from radial_back(
            0,
            jnp.concatenate([grads[0] * kept, towards * kept], axis=0),
            bas[a],
            act.at[a],
        )
        vector = vec[a]
        direct = nn(adds, jnp.concatenate([vector * g for g in grads[1:]], axis=0))
        moved = []
        for k in range(3):
            pulled = rel[k] * pull + direct[k : k + 1]
            if a == 0:
                pulled = pulled + drs[k : k + 1, :]
            moved.append(pulled / CELL)
            tgs[a, k : k + 1, :] = fold(moved[k])
        moved.append(jnp.zeros((1, EDGES), F32))
        moved = jnp.concatenate(moved * 4, axis=0).astype(BF16)
        spread = jnp.concatenate([moved] * 7, axis=0) * nqs[a]
        spreads.append(nt(spread, ohot[a]))

    tgs[...] = jnp.zeros((CHUNKS, 4, ATOMS), F32)
    spreads = []
    in_turns([backward_two()] + [backward(a) for a in (1, 2, 3, 4, 5, 6, 7, 0)], 3)
    pgs[...] = sum(spreads)

    pos_copies = []
    for d in itertools.product((-1, 0, 1), repeat=3):
        n = place(d)
        pgx[n] = pgs[n * 4 : n * 4 + 4, :] - jnp.where(lanes_of(d), tgs[chunk_of(d)], 0.0)
    for i, d in enumerate(NEIGHBOURS):
        there = place(tuple(-k for k in d))
        copy = remote(
            pgx.at[place(d), 0:3], pr.at[there, 0:3], pos_s.at[i], pos_r.at[i], d
        )
        copy.start()
        pos_copies.append(copy)
    pending += pos_copies
    e_copies = share(1, esy, gathered(2, esz, e_copies), sizes[0])
    e_copies = share(0, esx, gathered(1, esy, e_copies), 0)
    for copy in pos_copies:
        copy.wait_recv()
    total = pgx[mine, 0:3, :]
    for d in NEIGHBOURS:
        total = total + pr[place(d), 0:3, :]
    for i, (x, y, z) in enumerate(OWN_CELLS):
        for k in range(3):
            frc[k, x, y, z : z + 1, :] = -total[k : k + 1, i * 16 : i * 16 + 16]
    eng[...] = gathered(0, esx, e_copies) / float(ATOMS * sizes[0] * sizes[1] * sizes[2])
    for copy in pending:
        copy.wait_send()


def body(sizes, *args):
    hbm = pl.BlockSpec(memory_space=pltpu.HBM)
    vmem = pl.BlockSpec(memory_space=pltpu.VMEM)
    held = [pltpu.VMEM(a.shape, a.dtype) for a in args]
    held[2] = pltpu.SMEM(args[2].shape, args[2].dtype)
    energy_sends = sum(sizes)
    dma = pltpu.SemaphoreType.DMA
    scratch = [
        tuple(held),
        dma((len(args),)),
        pltpu.VMEM((27, 8, 128), F32),
        pltpu.VMEM((8, 8, 128), F32),
        pltpu.VMEM((112, 128), F32),
        pltpu.VMEM((8, 8, 128), jnp.int32),
        pltpu.VMEM((96, 128), F32),
        pltpu.VMEM((8, 8, 1024), F32),
        pltpu.VMEM((8, 3, 1024), F32),
        pltpu.VMEM((8, 112, 1024), BF16),
        pltpu.VMEM((8, 128, 1024), BF16),
        pltpu.VMEM((8, 128, 1024), BF16),
        pltpu.VMEM((256, 1024), F32),
        pltpu.VMEM((8, 2, 64, 1024), BF16),
        pltpu.VMEM((2, 64, 1024), BF16),
        pltpu.VMEM((8, 128, 1024), BF16),
        pltpu.VMEM((512, 1024), BF16),
        pltpu.VMEM((1024, 1024), BF16),
        pltpu.VMEM((1024, 1024), BF16),
        pltpu.VMEM((512, 1024), F32),
        pltpu.VMEM((512, 1024), BF16),
        pltpu.VMEM((512, 1024), BF16),
        pltpu.VMEM((8, 1024), F32),
        pltpu.VMEM((128, 128), BF16),
        pltpu.VMEM((112, 128), BF16),
        pltpu.VMEM((8, 4, 128), F32),
        pltpu.VMEM((112, 128), F32),
        pltpu.VMEM((27, 4, 128), F32),
        pltpu.VMEM((27, 4, 128), F32),
        pltpu.VMEM((sizes[0], 1, 128), F32),
        pltpu.VMEM((sizes[1], 1, 128), F32),
        pltpu.VMEM((sizes[2], 1, 128), F32),
        dma((26,)),
        dma((26,)),
        dma((26,)),
        dma((26,)),
        dma((energy_sends,)),
        dma((energy_sends,)),
    ]
    forces, energy = pl.pallas_call(
        functools.partial(kernel, sizes),
        out_shape=(
            jax.ShapeDtypeStruct(args[0].shape, F32),
            jax.ShapeDtypeStruct((1, 1), F32),
        ),
        in_specs=[hbm] * len(args),
        out_specs=(vmem, vmem),
        scratch_shapes=scratch,
        compiler_params=pltpu.CompilerParams(
            collective_id=0, has_side_effects=True, vmem_limit_bytes=62 * 1024 * 1024
        ),
    )(*args)
    return forces, energy.reshape(())


def solution(mesh):
    sizes = tuple(mesh.shape[a] for a in AXES)
    in_specs = (
        P(None, "gx", "gy", "gz", None),
        P("gx", "gy", "gz", None),
        P("gx", "gy", "gz"),
        P(None, "gx", "gy", "gz", None),
    ) + (P(),) * 8
    out_specs = (P(None, "gx", "gy", "gz", None), P())
    return jax.shard_map(
        functools.partial(body, sizes),
        mesh=mesh,
        in_specs=in_specs,
        out_specs=out_specs,
        check_vma=False,
    )
```
